32 devices in a mesh: groups: 2 (over y), expert: 4 (over z), hidden: 4 (over x, core).
Axes of the slice: x: 2, y: 2, z: 4, core: 2. Of those that a mesh axis runs over, the one named last changes fastest.
Arguments:
- tokens: bfloat16 [256, 3072], P(('groups', 'expert'), 'hidden'), parts along dimension 0, may hold values from -6 to 6
- router_weight: float32 [3072, 4], P('hidden'), may hold values from -0.109375 to 0.109375
- routes: int32 [256, 2], P(('groups', 'expert')), parts along dimension 0, may hold values from 0 to 3, as said below
- slots: int32 [256, 2], P(('groups', 'expert')), parts along dimension 0, may hold values from 0 to 127, as said below
- gate_weight: bfloat16 [4, 3072, 16384], P('expert', None, 'hidden'), may hold values from -0.109375 to 0.109375
- up_weight: bfloat16 [4, 3072, 16384], P('expert', None, 'hidden'), may hold values from -0.109375 to 0.109375
- down_weight: bfloat16 [4, 16384, 3072], P('expert', 'hidden'), may hold values from -0.0625 to 0.0625
- scale_exponents: int32 [8, 4, 128, 24], P(('groups', 'expert'), 'hidden'), parts along dimension 0, may hold values from 10 to 13
Outputs:
- mixed: bfloat16 [256, 3072], P(('groups', 'expert'), 'hidden'), parts along dimension 0
The draws below stay inside these ranges and needn't reach their ends.
There are 2 independent parts, one for each index of `groups`. The reference program is written for one: setup_inputs(seed, part) draws one part's arguments, and reference() takes and returns one part's arrays. A program takes and returns all parts, laid end to end along the dimension named above; an argument that names none is the same for every part. Nothing has to cross between parts.
Inputs may be any that keep to these rules, and one draw needn't show every extreme that they name: `routes`: each token names two different experts. For each expert the slots of the tokens routed to it are distinct; the tokens of rows i * 32 to (i + 1) * 32 - 1 have slots from i * 32 to (i + 1) * 32 - 1.
All inputs are finite; a program needn't handle non-finite values.
Results may differ from the reference program's by a relative error of at most 0.01.
Values may be sent and summed in bfloat16 or wider, within the bound.
No kernel may reach another device: no remote copies, remote signals or barrier semaphores. Data moves between devices by JAX's collectives and lax.ppermute only.
A program may use at most 192 MiB of HBM per device.

```python
import jax
import jax.numpy as jnp
from jax import lax

D = 3072
FF = 16384
EXPERTS = 4
TOK_DEV = 32
SLOTS = 32
TOKENS = 128
CAP = 128
GROUP = 1
BLOCKS = 24
N_EXPERT = 4
N_HIDDEN = 4


def route_tables(key):
    sources = TOKENS // TOK_DEV
    key_order, key_pick, key_step, key_place = jax.random.split(key, 4)
    order = jax.random.permutation(key_order, EXPERTS)
    pick = jax.random.randint(key_pick, (TOKENS,), 0, 16)
    level = (pick >= 8).astype(jnp.int32) + (pick >= 12).astype(jnp.int32) + (pick >= 14).astype(jnp.int32)
    level = jnp.minimum(level, EXPERTS - 1)
    first = order[level]
    step_by = jax.random.randint(key_step, (TOKENS,), 1, EXPERTS)
    second = (first + step_by) % EXPERTS
    routes = jnp.stack([first, second], axis=1).astype(jnp.int32)
    member = jnp.sum((routes[:, :, None] == jnp.arange(EXPERTS)[None, None, :]).astype(jnp.int32), axis=1)
    member = member.reshape(sources, TOK_DEV, EXPERTS)
    ranks = (jnp.cumsum(member, axis=1) - member).reshape(TOKENS, EXPERTS)
    scores = jax.random.randint(key_place, (sources, EXPERTS, SLOTS - 1), 0, 2 ** 30)
    others = jnp.argsort(scores, axis=-1).astype(jnp.int32)
    places = jnp.concatenate([jnp.full((sources, EXPERTS, 1), SLOTS - 1, jnp.int32), others], axis=-1)
    route_rank = jnp.take_along_axis(ranks, routes, axis=1)
    owner = (jnp.arange(TOKENS) // TOK_DEV).astype(jnp.int32)
    local = places[owner[:, None], routes, route_rank]
    slots = (owner[:, None] * SLOTS + local).astype(jnp.int32)
    return (routes, slots)


def draw_routes(key, part):
    tables = route_tables(key)
    return tables[0]


def draw_slots(key, part):
    tables = route_tables(key)
    return tables[1]


def plant(values, stream_key, least, top_value):
    dims = values.shape
    index_at = [jax.random.randint(jax.random.fold_in(stream_key, axis), (), 0, dims[axis]) for axis in range(len(dims))]
    values = values.at[tuple(index_at)].set(least)
    longest = dims.index(max(dims))
    index_at[longest] = (index_at[longest] + 1) % dims[longest]
    return values.at[tuple(index_at)].set(top_value)


def spiked(values, stream_key, source, target, blocks, factor):
    def block_of(dim):
        return (jnp.arange(values.shape[dim]) // (values.shape[dim] // blocks)).reshape((-1,) + (1,) * (values.ndim - 1 - dim))

    near = jax.random.permutation(stream_key, blocks)[block_of(target)]
    far = (block_of(target) + blocks // 2) % blocks
    return jnp.where((block_of(source) == near) | (block_of(source) == far), factor * values, values)


def steps_of(own_key, extent, cuts, low, largest):
    def one(dim, shards_of):
        steps = jax.random.uniform(jax.random.fold_in(jax.random.fold_in(own_key, 6), dim), (shards_of,), jnp.float32, low / len(cuts), largest / len(cuts))
        return jnp.repeat(jnp.exp(steps), extent[dim] // shards_of).reshape((-1,) + (1,) * (len(extent) - dim - 1))

    level = one(*cuts[0])
    for cut in cuts[1:]:
        level = level * one(*cut)
    return level


def bell_draw(rng, extent, deviation, reach, cuts=(), held_as=jnp.bfloat16):
    values = jax.random.normal(rng, extent, jnp.float32) * deviation
    if len(cuts) > 0:
        values = steps_of(rng, extent, cuts, -0.22, 0.18) * values
    return jnp.clip(values, min=-reach, max=reach).astype(held_as)


def gaussian_with(own_key, dims, spread, reach, cuts, heavy, kind=jnp.bfloat16):
    values = spread * jax.random.normal(own_key, dims, jnp.float32)
    if cuts:
        values = values * steps_of(own_key, dims, cuts, -0.22, 0.18)
    return jnp.clip(spiked(values, jax.random.fold_in(own_key, 3), *heavy), -reach, reach).astype(kind)


def setup_inputs(seed: int = 0, part: int = 0) -> dict:
    streams_of = jax.random.split(jax.random.key(seed), 9)
    own_keys = jax.random.split(jax.random.fold_in(streams_of[8], part), 9)
    tokens = bell_draw(own_keys[0], (TOKENS, D), 1.0, 6.0, ((0, 4), (1, 4)))
    router_weight = bell_draw(streams_of[1], (D, EXPERTS), D ** -0.5, 0.109375, ((0, 4),), jnp.float32)
    routes = draw_routes(jax.random.fold_in(jax.random.fold_in(streams_of[8], part), 71), part)
    slots = draw_slots(jax.random.fold_in(jax.random.fold_in(streams_of[8], part), 71), part)
    gate_weight = bell_draw(streams_of[4], (EXPERTS * GROUP, D, FF // GROUP), D ** -0.5, 0.109375, ((0, 4), (2, 4)))
    up_weight = bell_draw(streams_of[5], (EXPERTS * GROUP, D, FF // GROUP), D ** -0.5, 0.109375, ((0, 4), (2, 4)))
    down_weight = gaussian_with(streams_of[6], (EXPERTS * GROUP, FF // GROUP, D), FF ** -0.5, 0.0625, ((0, 4), (1, 4)), (1, 2, 4, 2.0))
    scale_exponents = plant(jax.random.randint(own_keys[7], (EXPERTS * GROUP, N_HIDDEN, CAP, BLOCKS), 10, 14), jax.random.fold_in(own_keys[7], 1), 10, 13).astype(jnp.int32)
    return dict(tokens=tokens, router_weight=router_weight, routes=routes, slots=slots, gate_weight=gate_weight, up_weight=up_weight, down_weight=down_weight, scale_exponents=scale_exponents)


def reference(tokens, router_weight, routes, slots, gate_weight, up_weight, down_weight, scale_exponents):
    group = N_EXPERT // EXPERTS
    hid_dev = FF // (group * N_HIDDEN)
    logits = jnp.dot(tokens.astype(jnp.float32), router_weight, precision=lax.Precision.HIGHEST)
    chosen = jnp.take_along_axis(logits, routes, axis=1)
    first_w = jax.nn.sigmoid(chosen[:, 0] - chosen[:, 1])
    second_w = jax.nn.sigmoid(chosen[:, 1] - chosen[:, 0])
    doubled = jnp.repeat(tokens, 2, axis=0)

    def one_expert(expert):
        target = jnp.where(routes == expert, slots, CAP).reshape(-1).astype(jnp.int32)
        buffer = jnp.zeros((CAP + 1, D), jnp.bfloat16).at[target].set(doubled)[:CAP]
        start = (expert * group).astype(jnp.int32)
        gate_full = lax.dynamic_slice_in_dim(gate_weight, start, group, 0).transpose(1, 0, 2).reshape(D, FF)
        up_full = lax.dynamic_slice_in_dim(up_weight, start, group, 0).transpose(1, 0, 2).reshape(D, FF)
        down_full = lax.dynamic_slice_in_dim(down_weight, start, group, 0).reshape(FF, D)
        exponents = lax.dynamic_slice_in_dim(scale_exponents, start, group, 0)
        gate = jnp.dot(buffer, gate_full, preferred_element_type=jnp.float32)
        up_val = jnp.dot(buffer, up_full, preferred_element_type=jnp.float32)
        hidden = (jax.nn.silu(gate) * up_val).astype(jnp.bfloat16)

        def quarter(index):
            def add_shard(shard, total):
                offset = ((index * N_HIDDEN + shard) * hid_dev).astype(jnp.int32)
                columns = lax.dynamic_slice_in_dim(hidden, offset, hid_dev, 1)
                rows_w = lax.dynamic_slice_in_dim(down_full, offset, hid_dev, 0)
                part = jnp.dot(columns, rows_w, preferred_element_type=jnp.float32)
                expo = exponents[index, shard]
                limit = 448.0 * jnp.exp2(-expo.astype(jnp.float32))[:, :, None]
                coded = jnp.clip(part.reshape(CAP, BLOCKS, 128), -limit, limit).astype(jnp.bfloat16)
                return total + coded.reshape(CAP, D).astype(jnp.float32)

            total = lax.fori_loop(0, N_HIDDEN, add_shard, jnp.zeros((CAP, D), jnp.float32))
            return total.astype(jnp.bfloat16)

        quarters = lax.map(quarter, jnp.arange(group, dtype=jnp.int32))
        return jnp.sum(quarters.astype(jnp.float32), axis=0)

    outputs = lax.map(one_expert, jnp.arange(EXPERTS, dtype=jnp.int32))
    first_rows = outputs[routes[:, 0], slots[:, 0]]
    second_rows = outputs[routes[:, 1], slots[:, 1]]
    mixed = first_w[:, None] * first_rows + second_w[:, None] * second_rows
    return mixed.astype(jnp.bfloat16)
```

```python
import functools

import jax
import jax.numpy as jnp
from jax import lax
from jax.experimental import pallas as pl
from jax.experimental.pallas import tpu as pltpu
from jax.sharding import PartitionSpec as P

EXPERTS = 4
LANES = 128
BF16 = jnp.bfloat16
F32 = jnp.float32
MIB = 1 << 20
JOINT = ("expert", "hidden")
VMEM = pl.BlockSpec(memory_space=pltpu.VMEM)
HBM = pl.BlockSpec(memory_space=pltpu.HBM)


def on_device(
    tokens, router_weight, routes, slots, gate_weight, up_weight, down_weight, scale_exponents
):
    slot_count = tokens.shape[0]
    width_dev = tokens.shape[1]
    group = lax.axis_size("expert") // EXPERTS
    source = lax.axis_index("expert")
    partial_logits = jnp.dot(
        tokens.astype(jnp.float32), router_weight, precision=lax.Precision.HIGHEST
    )
    logits = lax.psum(partial_logits, "hidden")
    expert_ids = jnp.arange(EXPERTS, dtype=jnp.int32)
    picked = (routes[:, :, None] == expert_ids[None, None, :]).astype(jnp.float32)
    chosen = jnp.sum(picked * logits[:, None, :], axis=2)
    first_w = jax.nn.sigmoid(chosen[:, 0] - chosen[:, 1])
    second_w = jax.nn.sigmoid(chosen[:, 1] - chosen[:, 0])
    route_w = jnp.stack([first_w, second_w], axis=1)
    local = slots - source * slot_count
    positions = jnp.arange(slot_count, dtype=jnp.int32)
    placed = (local[:, :, None] == positions[None, None, :]).astype(jnp.float32)
    select = jnp.einsum("tke,tks->est", picked, placed).astype(jnp.bfloat16)
    weighted = jnp.einsum("tke,tks,tk->est", picked, placed, route_w)
    gate_w = gate_weight[0]
    up_w = up_weight[0]
    whole = lax.all_gather(tokens, "hidden", axis=1, tiled=True)
    outgoing = jnp.einsum("est,td->esd", select, whole, preferred_element_type=jnp.float32).astype(
        jnp.bfloat16
    )
    outgoing = jnp.repeat(outgoing, group, axis=0)
    arrived = lax.all_to_all(outgoing, "expert", split_axis=0, concat_axis=0, tiled=True)
    rows_in = arrived.reshape(-1, arrived.shape[2])
    gate = jnp.dot(rows_in, gate_w, preferred_element_type=jnp.float32)
    up_val = jnp.dot(rows_in, up_w, preferred_element_type=jnp.float32)
    hidden = (jax.nn.silu(gate) * up_val).astype(jnp.bfloat16)
    partial_value = jnp.dot(hidden, down_weight[0], preferred_element_type=jnp.float32)
    capacity = partial_value.shape[0]
    features = partial_value.shape[1]
    limit = 448.0 * jnp.exp2(-scale_exponents[0, 0].astype(jnp.float32))[:, :, None]
    coded = jnp.clip(partial_value.reshape(capacity, features // 128, 128), -limit, limit).astype(
        jnp.bfloat16
    )
    coded = coded.reshape(capacity, features)
    summed = lax.psum_scatter(
        coded.astype(jnp.float32).astype(jnp.bfloat16), "hidden", scatter_dimension=1, tiled=True
    )
    quarter_out = summed.reshape(-1, slot_count, width_dev)
    returned = lax.all_to_all(quarter_out, "expert", split_axis=0, concat_axis=0, tiled=True)
    expert_out = jnp.sum(
        returned.astype(jnp.float32).reshape(EXPERTS, group, slot_count, width_dev), axis=1
    )
    mixed = jnp.einsum("est,esd->td", weighted, expert_out, precision=lax.Precision.HIGHEST)
    return mixed.astype(jnp.bfloat16)


def swap(value, expert_bits, hidden_bits):
    pairs = [
        (e * 4 + h, (e ^ expert_bits) * 4 + (h ^ hidden_bits)) for e in range(4) for h in range(4)
    ]
    return lax.ppermute(value, JOINT, pairs)


def pack_body(tok_ref, rw_ref, routes_ref, slots_ref, out_ref):
    rows, width = tok_ref.shape
    base = lax.axis_index("expert") * rows
    out_ref[:, :width] = tok_ref[...]
    values = tok_ref[...].astype(F32)
    lane = lax.broadcasted_iota(jnp.int32, (rows, LANES), 1)
    diagonal = lax.broadcasted_iota(jnp.int32, (rows, rows), 0) == lax.broadcasted_iota(
        jnp.int32, (rows, rows), 1
    )
    meta = jnp.zeros((rows, LANES), F32)
    for expert in range(EXPERTS):
        logit = jnp.sum(values * rw_ref[expert : expert + 1, :], axis=1, keepdims=True)
        high = logit.astype(BF16).astype(F32)
        middle = (logit - high).astype(BF16).astype(F32)
        low = logit - high - middle
        code = jnp.zeros((1, rows), F32) - 1.0
        for pick in range(2):
            here = (slots_ref[pick : pick + 1, :] - base).astype(F32)
            code = jnp.where(routes_ref[pick : pick + 1, :] == expert, here, code)
        column = jnp.sum(jnp.where(diagonal, code, 0.0), axis=1, keepdims=True)
        for place, term in enumerate((column, high, middle, low)):
            meta = jnp.where(lane == place * EXPERTS + expert, term, meta)
    out_ref[:, width:] = meta.astype(BF16)


def pack(tokens, router_t, routes_t, slots_t):
    rows, width = tokens.shape
    return pl.pallas_call(
        pack_body,
        in_specs=[VMEM] * 4,
        out_specs=VMEM,
        out_shape=jax.ShapeDtypeStruct((rows, width + LANES), BF16),
        name="pack",
    )(tokens, router_t, routes_t, slots_t)


def join_body(*refs):
    out_ref = refs[-1]
    rows = refs[0].shape[0]
    for index, ref in enumerate(refs[:-1]):
        out_ref[index * rows : (index + 1) * rows, :] = ref[...]


def join(parts):
    rows, width = parts[0].shape
    return pl.pallas_call(
        join_body,
        in_specs=[VMEM] * len(parts),
        out_specs=VMEM,
        out_shape=jax.ShapeDtypeStruct((rows * len(parts), width), BF16),
        name="join",
    )(*parts)


def place():
    hidden = lax.axis_index("hidden")
    return hidden // 2, hidden % 2


def fill_left(left, first, second, core, width):
    left[:, pl.ds(pl.multiple_of(core * width, LANES), width)] = first[:, :width]
    left[:, pl.ds(pl.multiple_of((1 - core) * width, LANES), width)] = second[:, :width]


NEAR_TILE = 512
NEAR_SLOTS = 4


def near_body(own, mate, wg, wu, acc_g, acc_u, left, buf_g, buf_u, sem_g, sem_u):
    chip, core = place()
    width = own.shape[1] - LANES
    depth = 2 * width
    tiles = wg.shape[2] // NEAR_TILE

    def copies(index):
        slot = lax.rem(index, NEAR_SLOTS)
        rows = pl.ds(pl.multiple_of(chip * depth, LANES), depth)
        columns = pl.ds(pl.multiple_of(index * NEAR_TILE, NEAR_TILE), NEAR_TILE)
        return (
            pltpu.make_async_copy(wg.at[0, rows, columns], buf_g.at[slot], sem_g.at[slot]),
            pltpu.make_async_copy(wu.at[0, rows, columns], buf_u.at[slot], sem_u.at[slot]),
        )

    for index in range(NEAR_SLOTS):
        for copy in copies(index):
            copy.start()
    fill_left(left, own, mate, core, width)

    @pl.loop(0, tiles)
    def _(index):
        slot = lax.rem(index, NEAR_SLOTS)
        columns = pl.ds(pl.multiple_of(index * NEAR_TILE, NEAR_TILE), NEAR_TILE)
        copy_g, copy_u = copies(index)
        copy_g.wait()
        acc_g[:, columns] = jnp.dot(left[...], buf_g[slot], preferred_element_type=F32)
        copy_u.wait()
        acc_u[:, columns] = jnp.dot(left[...], buf_u[slot], preferred_element_type=F32)

        @pl.when(index + NEAR_SLOTS < tiles)
        def _():
            for copy in copies(index + NEAR_SLOTS):
                copy.start()


def near(own, mate, wg, wu):
    rows, width = own.shape
    depth = 2 * (width - LANES)
    units = wg.shape[2]
    acc = pltpu.VMEM((rows, units), F32)
    tile = pltpu.VMEM((NEAR_SLOTS, depth, NEAR_TILE), BF16)
    return pl.pallas_call(
        near_body,
        in_specs=[VMEM, VMEM, HBM, HBM],
        out_specs=[VMEM, VMEM],
        out_shape=[acc, acc],
        scratch_shapes=[
            pltpu.VMEM((rows, depth), BF16),
            tile,
            tile,
            pltpu.SemaphoreType.DMA((NEAR_SLOTS,)),
            pltpu.SemaphoreType.DMA((NEAR_SLOTS,)),
        ],
        cost_estimate=pl.CostEstimate(
            flops=4 * rows * depth * units, bytes_accessed=4 * depth * units, transcendentals=0
        ),
        compiler_params=pltpu.CompilerParams(vmem_limit_bytes=48 * MIB),
        name="near",
    )(own, mate, wg, wu)


FAR_TILE = 512
FAR_SLOTS = 4
DOWN_TILE = 384
DOWN_SLOTS = 4


def far_body(
    own, mate, cross, cross_mate, acc_g, acc_u, expo, wg, wu, wd, send, keep,
    left, hid, limits, share, buf_g, buf_u, buf_d, sem_g, sem_u, sem_d,
):
    chip, core = place()
    expert = lax.axis_index("expert")
    rows = own.shape[0]
    width = own.shape[1] - LANES
    depth = 2 * width
    tiles = wg.shape[2] // FAR_TILE
    parts = width // DOWN_TILE
    half = 2 * parts
    down_tiles = 2 * half

    def copies(index):
        slot = lax.rem(index, FAR_SLOTS)
        there = pl.ds(pl.multiple_of((1 - chip) * depth, LANES), depth)
        columns = pl.ds(pl.multiple_of(index * FAR_TILE, FAR_TILE), FAR_TILE)
        return (
            pltpu.make_async_copy(wg.at[0, there, columns], buf_g.at[slot], sem_g.at[slot]),
            pltpu.make_async_copy(wu.at[0, there, columns], buf_u.at[slot], sem_u.at[slot]),
        )

    def owner(index):
        block = index // parts
        to_chip = jnp.where(lax.rem(block, 2) == 0, chip, 1 - chip)
        to_core = jnp.where(block < 2, 1 - core, core)
        return 2 * to_chip + to_core

    def down_copy(index):
        slot = lax.rem(index, DOWN_SLOTS)
        start = owner(index) * width + lax.rem(index, parts) * DOWN_TILE
        columns = pl.ds(pl.multiple_of(start, LANES), DOWN_TILE)
        return pltpu.make_async_copy(wd.at[0, :, columns], buf_d.at[slot], sem_d.at[slot])

    for index in range(FAR_SLOTS):
        for copy in copies(index):
            copy.start()
    fill_left(left, cross, cross_mate, core, width)

    meta = own[:, width:].astype(F32)
    lane = lax.broadcasted_iota(jnp.int32, meta.shape, 1)
    terms = meta
    for ref in (mate, cross, cross_mate):
        terms = terms + ref[:, width:].astype(F32)

    def column(table, index):
        return jnp.sum(jnp.where(lane == index, table, 0.0), axis=1, keepdims=True)

    code = column(meta, expert)
    first = jnp.zeros((rows, 1), F32)
    other = jnp.zeros((rows, 1), F32)
    for index in range(EXPERTS):
        used = (lane >= EXPERTS) & (lane < 4 * EXPERTS) & (lax.rem(lane, EXPERTS) == index)
        logit = jnp.sum(jnp.where(used, terms, 0.0), axis=1, keepdims=True)
        routed = meta[:, index : index + 1] >= 0.0
        first = jnp.where(index == expert, logit, first)
        other = jnp.where(routed & (index != expert), logit, other)
    weight = jnp.where(code >= 0.0, 1.0 / (1.0 + jnp.exp(other - first)), 0.0)
    share[...] = jnp.broadcast_to(weight, share.shape)
    slots_each = rows // EXPERTS
    row = lax.broadcasted_iota(jnp.int32, (rows, rows), 0)
    source = jnp.bitwise_xor(row // slots_each, expert)
    target = jnp.where(code >= 0.0, (source * slots_each).astype(F32) + code, -1.0)
    chosen = lax.broadcasted_iota(jnp.int32, (rows, rows), 1).astype(F32) == target
    table = 448.0 * jnp.exp2(-expo[...].astype(F32))
    limit = lax.dot_general(
        chosen.astype(BF16), table.astype(BF16), (((1,), (1,)), ((), ())), preferred_element_type=F32
    )
    for index in range(limits.shape[0]):
        limits[index] = jnp.broadcast_to(limit[:, index : index + 1], (rows, LANES))

    @pl.loop(0, tiles)
    def _(index):
        slot = lax.rem(index, FAR_SLOTS)
        columns = pl.ds(pl.multiple_of(index * FAR_TILE, FAR_TILE), FAR_TILE)
        copy_g, copy_u = copies(index)
        copy_g.wait()
        gate = acc_g[:, columns] + jnp.dot(left[...], buf_g[slot], preferred_element_type=F32)
        copy_u.wait()
        up = acc_u[:, columns] + jnp.dot(left[...], buf_u[slot], preferred_element_type=F32)
        hid[:, columns] = (gate / (1.0 + jnp.exp(-gate)) * up).astype(BF16)

        @pl.when(index + FAR_SLOTS < tiles)
        def _():
            for copy in copies(index + FAR_SLOTS):
                copy.start()

        @pl.when(index + DOWN_SLOTS >= tiles)
        def _():
            down_copy(index + DOWN_SLOTS - tiles).start()

    def down(index, out, block):
        down_copy(index).wait()
        partial = jnp.dot(hid[...], buf_d[lax.rem(index, DOWN_SLOTS)], preferred_element_type=F32)
        pieces = []
        for piece in range(DOWN_TILE // LANES):
            feature = (owner(index) * width + lax.rem(index, parts) * DOWN_TILE) // LANES + piece
            bound = limits[feature]
            value = partial[:, piece * LANES : (piece + 1) * LANES]
            coded = jnp.clip(value, -bound, bound).astype(BF16).astype(F32)
            pieces.append(coded * share[...])
        columns = pl.ds(pl.multiple_of(lax.rem(index, parts) * DOWN_TILE, LANES), DOWN_TILE)
        out[block, :, columns] = jnp.concatenate(pieces, axis=1).astype(out.dtype)

        @pl.when(index + DOWN_SLOTS < down_tiles)
        def _():
            down_copy(index + DOWN_SLOTS).start()

    @pl.loop(0, half)
    def _(index):
        down(index, send, index // parts)

    @pl.loop(0, half)
    def _(index):
        down(index + half, keep, index // parts)


def far(own, mate, cross, cross_mate, acc_g, acc_u, expo, wg, wu, wd):
    rows, width = own.shape
    width = width - LANES
    depth = 2 * width
    units = wg.shape[2]
    tile = pltpu.VMEM((FAR_SLOTS, depth, FAR_TILE), BF16)
    return pl.pallas_call(
        far_body,
        in_specs=[VMEM] * 7 + [HBM] * 3,
        out_specs=[VMEM, VMEM],
        out_shape=[
            jax.ShapeDtypeStruct((2, rows, width), BF16),
            jax.ShapeDtypeStruct((2, rows, width), F32),
        ],
        scratch_shapes=[
            pltpu.VMEM((rows, depth), BF16),
            pltpu.VMEM((rows, units), BF16),
            pltpu.VMEM((expo.shape[0], rows, LANES), F32),
            pltpu.VMEM((rows, LANES), F32),
            tile,
            tile,
            pltpu.VMEM((DOWN_SLOTS, units, DOWN_TILE), BF16),
            pltpu.SemaphoreType.DMA((FAR_SLOTS,)),
            pltpu.SemaphoreType.DMA((FAR_SLOTS,)),
            pltpu.SemaphoreType.DMA((DOWN_SLOTS,)),
        ],
        cost_estimate=pl.CostEstimate(
            flops=8 * rows * depth * units, bytes_accessed=8 * depth * units, transcendentals=0
        ),
        compiler_params=pltpu.CompilerParams(vmem_limit_bytes=48 * MIB),
        name="far",
    )(own, mate, cross, cross_mate, acc_g, acc_u, expo, wg, wu, wd)


def split_body(keep, got, *outs):
    rows = outs[0].shape[0]
    for index, out in enumerate(outs):
        chip, block = index // EXPERTS, index % EXPERTS
        piece = slice(block * rows, (block + 1) * rows)
        out[...] = (keep[chip, piece, :] + got[chip, piece, :].astype(F32)).astype(out.dtype)


def split(keep, got):
    rows, width = keep.shape[1] // EXPERTS, keep.shape[2]
    kinds = [F32] + [BF16] * (2 * EXPERTS - 1)
    return pl.pallas_call(
        split_body,
        in_specs=[VMEM, VMEM],
        out_specs=[VMEM] * len(kinds),
        out_shape=[jax.ShapeDtypeStruct((rows, width), kind) for kind in kinds],
        name="split",
    )(keep, got)


def total_body(*refs):
    total = refs[0][...]
    for ref in refs[1:-1]:
        total = total + ref[...].astype(F32)
    refs[-1][...] = total.astype(BF16)


def total(parts):
    return pl.pallas_call(
        total_body,
        in_specs=[VMEM] * len(parts),
        out_specs=VMEM,
        out_shape=jax.ShapeDtypeStruct(parts[0].shape, BF16),
        name="total",
    )(*parts)


def fast(tokens, router_weight, routes, slots, gate_weight, up_weight, down_weight, scale_exponents):
    packed = pack(tokens, router_weight.T, routes.T, slots.T)
    own = join([packed] + [swap(packed, bits, 0) for bits in (1, 2, 3)])
    mate = swap(own, 0, 1)
    cross = swap(own, 0, 2)
    acc_g, acc_u = near(own, mate, gate_weight, up_weight)
    cross_mate = swap(cross, 0, 1)
    send, keep = far(
        own, mate, cross, cross_mate, acc_g, acc_u, scale_exponents[0, 0].T,
        gate_weight, up_weight, down_weight,
    )
    got = swap(send, 0, 1)
    blocks = split(keep, got)
    parts = [blocks[0]]
    for bits in (3, 2, 1):
        for chip in (2, 0):
            parts.append(swap(blocks[(chip // 2) * EXPERTS + bits], bits, chip))
    parts.append(swap(blocks[EXPERTS], 0, 2))
    return total(parts)


def solution(mesh):
    placed = (
        P(("groups", "expert"), "hidden"),
        P("hidden", None),
        P(("groups", "expert"), None),
        P(("groups", "expert"), None),
        P("expert", None, "hidden"),
        P("expert", None, "hidden"),
        P("expert", "hidden", None),
        P(("groups", "expert"), "hidden", None, None),
    )
    general = mesh.shape["expert"] != 4 or mesh.shape["hidden"] != 4
    return jax.shard_map(
        on_device if general else fast,
        mesh=mesh,
        in_specs=placed,
        out_specs=P(("groups", "expert"), "hidden"),
        check_vma=False,
    )
```

```python
import functools

import jax
import jax.numpy as jnp
from jax import lax
from jax.experimental import pallas as pl
from jax.experimental.pallas import tpu as pltpu
from jax.sharding import PartitionSpec as P

EXPERTS = 4
LANES = 128
BF16 = jnp.bfloat16
F32 = jnp.float32
MIB = 1 << 20
JOINT = ("expert", "hidden")
VMEM = pl.BlockSpec(memory_space=pltpu.VMEM)
HBM = pl.BlockSpec(memory_space=pltpu.HBM)


def on_device(
    tokens, router_weight, routes, slots, gate_weight, up_weight, down_weight, scale_exponents
):
    slot_count = tokens.shape[0]
    width_dev = tokens.shape[1]
    group = lax.axis_size("expert") // EXPERTS
    source = lax.axis_index("expert")
    partial_logits = jnp.dot(
        tokens.astype(jnp.float32), router_weight, precision=lax.Precision.HIGHEST
    )
    logits = lax.psum(partial_logits, "hidden")
    expert_ids = jnp.arange(EXPERTS, dtype=jnp.int32)
    picked = (routes[:, :, None] == expert_ids[None, None, :]).astype(jnp.float32)
    chosen = jnp.sum(picked * logits[:, None, :], axis=2)
    first_w = jax.nn.sigmoid(chosen[:, 0] - chosen[:, 1])
    second_w = jax.nn.sigmoid(chosen[:, 1] - chosen[:, 0])
    route_w = jnp.stack([first_w, second_w], axis=1)
    local = slots - source * slot_count
    positions = jnp.arange(slot_count, dtype=jnp.int32)
    placed = (local[:, :, None] == positions[None, None, :]).astype(jnp.float32)
    select = jnp.einsum("tke,tks->est", picked, placed).astype(jnp.bfloat16)
    weighted = jnp.einsum("tke,tks,tk->est", picked, placed, route_w)
    gate_w = gate_weight[0]
    up_w = up_weight[0]
    whole = lax.all_gather(tokens, "hidden", axis=1, tiled=True)
    outgoing = jnp.einsum("est,td->esd", select, whole, preferred_element_type=jnp.float32).astype(
        jnp.bfloat16
    )
    outgoing = jnp.repeat(outgoing, group, axis=0)
    arrived = lax.all_to_all(outgoing, "expert", split_axis=0, concat_axis=0, tiled=True)
    rows_in = arrived.reshape(-1, arrived.shape[2])
    gate = jnp.dot(rows_in, gate_w, preferred_element_type=jnp.float32)
    up_val = jnp.dot(rows_in, up_w, preferred_element_type=jnp.float32)
    hidden = (jax.nn.silu(gate) * up_val).astype(jnp.bfloat16)
    partial_value = jnp.dot(hidden, down_weight[0], preferred_element_type=jnp.float32)
    capacity = partial_value.shape[0]
    features = partial_value.shape[1]
    limit = 448.0 * jnp.exp2(-scale_exponents[0, 0].astype(jnp.float32))[:, :, None]
    coded = jnp.clip(partial_value.reshape(capacity, features // 128, 128), -limit, limit).astype(
        jnp.bfloat16
    )
    coded = coded.reshape(capacity, features)
    summed = lax.psum_scatter(
        coded.astype(jnp.float32).astype(jnp.bfloat16), "hidden", scatter_dimension=1, tiled=True
    )
    quarter_out = summed.reshape(-1, slot_count, width_dev)
    returned = lax.all_to_all(quarter_out, "expert", split_axis=0, concat_axis=0, tiled=True)
    expert_out = jnp.sum(
        returned.astype(jnp.float32).reshape(EXPERTS, group, slot_count, width_dev), axis=1
    )
    mixed = jnp.einsum("est,esd->td", weighted, expert_out, precision=lax.Precision.HIGHEST)
    return mixed.astype(jnp.bfloat16)


def swap(value, expert_bits, hidden_bits):
    pairs = [
        (e * 4 + h, (e ^ expert_bits) * 4 + (h ^ hidden_bits)) for e in range(4) for h in range(4)
    ]
    return lax.ppermute(value, JOINT, pairs)


def in_vmem(array):
    return pltpu.with_memory_space_constraint(array, pltpu.VMEM)


def in_hbm(array):
    return pltpu.with_memory_space_constraint(array, pltpu.HBM)


def pack_body(tokens, router, routes, slots, out_ref, tok_ref, rw_ref, routes_ref, slots_ref, sem):
    rows, width = tok_ref.shape
    base = lax.axis_index("expert") * rows
    moves = ((tokens, tok_ref), (router, rw_ref), (routes, routes_ref), (slots, slots_ref))
    copies = [pltpu.make_async_copy(*move, sem.at[index]) for index, move in enumerate(moves)]
    for copy in copies:
        copy.start()
    for copy in copies:
        copy.wait()
    out_ref[:, :width] = tok_ref[...]
    values = tok_ref[...].astype(F32)
    lane = lax.broadcasted_iota(jnp.int32, (rows, LANES), 1)
    diagonal = lax.broadcasted_iota(jnp.int32, (rows, rows), 0) == lax.broadcasted_iota(
        jnp.int32, (rows, rows), 1
    )
    meta = jnp.zeros((rows, LANES), F32)
    for expert in range(EXPERTS):
        logit = jnp.sum(values * rw_ref[expert : expert + 1, :], axis=1, keepdims=True)
        high = logit.astype(BF16).astype(F32)
        middle = (logit - high).astype(BF16).astype(F32)
        low = logit - high - middle
        code = jnp.zeros((1, rows), F32) - 1.0
        for pick in range(2):
            here = (slots_ref[pick : pick + 1, :] - base).astype(F32)
            code = jnp.where(routes_ref[pick : pick + 1, :] == expert, here, code)
        column = jnp.sum(jnp.where(diagonal, code, 0.0), axis=1, keepdims=True)
        for place, term in enumerate((column, high, middle, low)):
            meta = jnp.where(lane == place * EXPERTS + expert, term, meta)
    out_ref[:, width:] = meta.astype(BF16)


PACK_FLOPS = 24_000_000_000


def pack(tokens, router_t, routes_t, slots_t):
    rows, width = tokens.shape
    arrays = [in_hbm(array) for array in (tokens, router_t, routes_t, slots_t)]
    return pl.pallas_call(
        pack_body,
        in_specs=[HBM] * 4,
        out_specs=VMEM,
        out_shape=pltpu.VMEM((rows, width + LANES), BF16),
        scratch_shapes=[pltpu.VMEM(array.shape, array.dtype) for array in arrays]
        + [pltpu.SemaphoreType.DMA((4,))],
        compiler_params=pltpu.CompilerParams(vmem_limit_bytes=4 * MIB),
        cost_estimate=pl.CostEstimate(flops=PACK_FLOPS, bytes_accessed=0, transcendentals=0),
        name="pack",
    )(*arrays)


def join_body(*refs):
    out_ref = refs[-1]
    rows = refs[0].shape[0]
    for index, ref in enumerate(refs[:-1]):
        out_ref[index * rows : (index + 1) * rows, :] = ref[...]


def join(parts):
    rows, width = parts[0].shape
    return pl.pallas_call(
        join_body,
        in_specs=[VMEM] * len(parts),
        out_specs=VMEM,
        out_shape=pltpu.VMEM((rows * len(parts), width), BF16),
        compiler_params=pltpu.CompilerParams(vmem_limit_bytes=4 * MIB),
        name="join",
    )(*parts)


def place():
    hidden = lax.axis_index("hidden")
    return hidden // 2, hidden % 2


TILE = 512


def span(index, size):
    return pl.ds(pl.multiple_of(index * size, size), size)


SCOPE = 13 * MIB
SLOTS = 6
CUT = 1024
SUB = 256


def main_body(
    own, mate, cross, cross_mate, expo, wg, wu, wd, send, keep, left, hid, limits, buf, sem
):
    chip, core = place()
    expert = lax.axis_index("expert")
    rows = own.shape[0]
    width = own.shape[1] - LANES
    slots = buf.shape[0]
    cuts = hid.shape[1] // CUT

    def owner(block):
        to_chip = chip if block % 2 == 0 else 1 - chip
        return 2 * to_chip + (1 - core if block < 2 else core)

    def copy(unit):
        part = wd.at[0, pl.ds(unit % cuts * CUT, CUT), span(owner(unit // cuts), width)]
        return pltpu.make_async_copy(part, buf.at[unit % slots], sem.at[unit % slots])

    for unit in range(slots):
        copy(unit).start()

    for to_chip, first, second in ((chip, own, mate), (1 - chip, cross, cross_mate)):
        left[:, span(2 * to_chip + core, width)] = first[:, :width]
        left[:, span(2 * to_chip + 1 - core, width)] = second[:, :width]

    meta = own[:, width:].astype(F32)
    lane = lax.broadcasted_iota(jnp.int32, meta.shape, 1)
    terms = meta
    for ref in (mate, cross, cross_mate):
        terms = terms + ref[:, width:].astype(F32)
    code = jnp.sum(jnp.where(lane == expert, meta, 0.0), axis=1, keepdims=True)
    first = jnp.zeros((rows, 1), F32)
    other = jnp.zeros((rows, 1), F32)
    for index in range(EXPERTS):
        used = (lane >= EXPERTS) & (lane < 4 * EXPERTS) & (lax.rem(lane, EXPERTS) == index)
        logit = jnp.sum(jnp.where(used, terms, 0.0), axis=1, keepdims=True)
        routed = meta[:, index : index + 1] >= 0.0
        first = jnp.where(index == expert, logit, first)
        other = jnp.where(routed & (index != expert), logit, other)
    weight = jnp.where(code >= 0.0, 1.0 / (1.0 + jnp.exp(other - first)), 0.0)
    slots_each = rows // EXPERTS
    row = lax.broadcasted_iota(jnp.int32, (rows, rows), 0)
    source = jnp.bitwise_xor(row // slots_each, expert)
    target = jnp.where(code >= 0.0, (source * slots_each).astype(F32) + code, -1.0)
    chosen = lax.broadcasted_iota(jnp.int32, (rows, rows), 1).astype(F32) == target
    table = 448.0 * jnp.exp2(-expo[...].astype(F32))
    limits[...] = lax.dot_general(
        chosen.astype(BF16), table.astype(BF16), (((1,), (1,)), ((), ())), preferred_element_type=F32
    )

    @pl.loop(0, wg.shape[1] // TILE)
    def _(index):
        for sub in range(TILE // SUB):
            columns = span(index * (TILE // SUB) + sub, SUB)
            gate = jnp.dot(left[...], wg[:, columns], preferred_element_type=F32)
            up = jnp.dot(left[...], wu[:, columns], preferred_element_type=F32)
            hid[:, columns] = (gate / (1.0 + jnp.exp(-gate)) * up).astype(BF16)

    unit = 0
    for block in range(4):
        partial = None
        for cut in range(cuts):
            copy(unit).wait()
            term = jnp.dot(
                hid[:, cut * CUT : (cut + 1) * CUT], buf[unit % slots], preferred_element_type=F32
            )
            partial = term if partial is None else partial + term
            if unit + slots < 4 * cuts:
                copy(unit + slots).start()
            unit += 1
        out = (send, keep)[block // 2]
        blocks = lax.broadcasted_iota(jnp.int32, limits.shape, 1)
        for piece in range(width // LANES):
            columns = slice(piece * LANES, (piece + 1) * LANES)
            feature = owner(block) * (width // LANES) + piece
            bound = jnp.sum(jnp.where(blocks == feature, limits[...], 0.0), axis=1, keepdims=True)
            coded = jnp.clip(partial[:, columns], -bound, bound).astype(BF16).astype(F32)
            out[block % 2, :, columns] = (coded * weight).astype(out.dtype)


def main(own, mate, cross, cross_mate, expo, wg, wu, wd):
    rows, width = own.shape
    width = width - LANES
    depth, units = wg.shape
    return pl.pallas_call(
        main_body,
        in_specs=[VMEM] * 7 + [HBM],
        out_specs=[VMEM, VMEM],
        out_shape=[pltpu.VMEM((2, rows, width), BF16), pltpu.VMEM((2, rows, width), F32)],
        scratch_shapes=[
            pltpu.VMEM((rows, depth), BF16),
            pltpu.VMEM((rows, units), BF16),
            pltpu.VMEM((rows, expo.shape[0]), F32),
            pltpu.VMEM((SLOTS, CUT, width), BF16),
            pltpu.SemaphoreType.DMA((SLOTS,)),
        ],
        cost_estimate=pl.CostEstimate(
            flops=6 * rows * depth * units, bytes_accessed=6 * depth * units, transcendentals=0
        ),
        compiler_params=pltpu.CompilerParams(vmem_limit_bytes=SCOPE),
        name="main",
    )(own, mate, cross, cross_mate, expo, wg, wu, wd)


def split_body(keep, got, *outs):
    rows = outs[0].shape[0]
    for index, out in enumerate(outs):
        chip, block = index // EXPERTS, index % EXPERTS
        piece = slice(block * rows, (block + 1) * rows)
        out[...] = (keep[chip, piece, :] + got[chip, piece, :].astype(F32)).astype(out.dtype)


def split(keep, got):
    rows, width = keep.shape[1] // EXPERTS, keep.shape[2]
    kinds = [F32] + [BF16] * (2 * EXPERTS - 1)
    return pl.pallas_call(
        split_body,
        in_specs=[VMEM, VMEM],
        out_specs=[VMEM] * len(kinds),
        out_shape=[jax.ShapeDtypeStruct((rows, width), kind) for kind in kinds],
        compiler_params=pltpu.CompilerParams(vmem_limit_bytes=4 * MIB),
        name="split",
    )(keep, got)


def total_body(*refs):
    total = refs[0][...]
    for ref in refs[1:-1]:
        total = total + ref[...].astype(F32)
    refs[-1][...] = total.astype(BF16)


def total(parts):
    return pl.pallas_call(
        total_body,
        in_specs=[VMEM] * len(parts),
        out_specs=VMEM,
        out_shape=jax.ShapeDtypeStruct(parts[0].shape, BF16),
        compiler_params=pltpu.CompilerParams(vmem_limit_bytes=4 * MIB),
        name="total",
    )(*parts)


def fast(tokens, router_weight, routes, slots, gate_weight, up_weight, down_weight, scale_exponents):
    packed = pack(tokens, router_weight.T, routes.T, slots.T)
    own = in_vmem(join([packed] + [swap(packed, bits, 0) for bits in (1, 2, 3)]))
    mate = in_vmem(swap(own, 0, 1))
    cross = in_vmem(swap(own, 0, 2))
    cross_mate = in_vmem(swap(cross, 0, 1))
    send, keep = main(
        own, mate, cross, cross_mate, in_vmem(scale_exponents[0, 0].T),
        in_vmem(gate_weight[0]), in_vmem(up_weight[0]), in_hbm(down_weight),
    )
    blocks = split(in_vmem(keep), in_vmem(swap(send, 0, 1)))
    parts = [blocks[0]]
    for bits in (3, 2, 1):
        for chip in (2, 0):
            parts.append(swap(blocks[(chip // 2) * EXPERTS + bits], bits, chip))
    parts.append(swap(blocks[EXPERTS], 0, 2))
    return total(parts)


def solution(mesh):
    placed = (
        P(("groups", "expert"), "hidden"),
        P("hidden", None),
        P(("groups", "expert"), None),
        P(("groups", "expert"), None),
        P("expert", None, "hidden"),
        P("expert", None, "hidden"),
        P("expert", "hidden", None),
        P(("groups", "expert"), "hidden", None, None),
    )
    general = mesh.shape["expert"] != 4 or mesh.shape["hidden"] != 4
    return jax.shard_map(
        on_device if general else fast,
        mesh=mesh,
        in_specs=placed,
        out_specs=P(("groups", "expert"), "hidden"),
        check_vma=False,
    )
```

```python
import functools

import jax
import jax.numpy as jnp
from jax import lax
from jax.experimental import pallas as pl
from jax.experimental.pallas import tpu as pltpu
from jax.sharding import PartitionSpec as P

EXPERTS = 4
LANES = 128
BF16 = jnp.bfloat16
F32 = jnp.float32
MIB = 1 << 20
JOINT = ("expert", "hidden")
VMEM = pl.BlockSpec(memory_space=pltpu.VMEM)
HBM = pl.BlockSpec(memory_space=pltpu.HBM)


def on_device(
    tokens, router_weight, routes, slots, gate_weight, up_weight, down_weight, scale_exponents
):
    slot_count = tokens.shape[0]
    width_dev = tokens.shape[1]
    group = lax.axis_size("expert") // EXPERTS
    source = lax.axis_index("expert")
    partial_logits = jnp.dot(
        tokens.astype(jnp.float32), router_weight, precision=lax.Precision.HIGHEST
    )
    logits = lax.psum(partial_logits, "hidden")
    expert_ids = jnp.arange(EXPERTS, dtype=jnp.int32)
    picked = (routes[:, :, None] == expert_ids[None, None, :]).astype(jnp.float32)
    chosen = jnp.sum(picked * logits[:, None, :], axis=2)
    first_w = jax.nn.sigmoid(chosen[:, 0] - chosen[:, 1])
    second_w = jax.nn.sigmoid(chosen[:, 1] - chosen[:, 0])
    route_w = jnp.stack([first_w, second_w], axis=1)
    local = slots - source * slot_count
    positions = jnp.arange(slot_count, dtype=jnp.int32)
    placed = (local[:, :, None] == positions[None, None, :]).astype(jnp.float32)
    select = jnp.einsum("tke,tks->est", picked, placed).astype(jnp.bfloat16)
    weighted = jnp.einsum("tke,tks,tk->est", picked, placed, route_w)
    gate_w = gate_weight[0]
    up_w = up_weight[0]
    whole = lax.all_gather(tokens, "hidden", axis=1, tiled=True)
    outgoing = jnp.einsum("est,td->esd", select, whole, preferred_element_type=jnp.float32).astype(
        jnp.bfloat16
    )
    outgoing = jnp.repeat(outgoing, group, axis=0)
    arrived = lax.all_to_all(outgoing, "expert", split_axis=0, concat_axis=0, tiled=True)
    rows_in = arrived.reshape(-1, arrived.shape[2])
    gate = jnp.dot(rows_in, gate_w, preferred_element_type=jnp.float32)
    up_val = jnp.dot(rows_in, up_w, preferred_element_type=jnp.float32)
    hidden = (jax.nn.silu(gate) * up_val).astype(jnp.bfloat16)
    partial_value = jnp.dot(hidden, down_weight[0], preferred_element_type=jnp.float32)
    capacity = partial_value.shape[0]
    features = partial_value.shape[1]
    limit = 448.0 * jnp.exp2(-scale_exponents[0, 0].astype(jnp.float32))[:, :, None]
    coded = jnp.clip(partial_value.reshape(capacity, features // 128, 128), -limit, limit).astype(
        jnp.bfloat16
    )
    coded = coded.reshape(capacity, features)
    summed = lax.psum_scatter(
        coded.astype(jnp.float32).astype(jnp.bfloat16), "hidden", scatter_dimension=1, tiled=True
    )
    quarter_out = summed.reshape(-1, slot_count, width_dev)
    returned = lax.all_to_all(quarter_out, "expert", split_axis=0, concat_axis=0, tiled=True)
    expert_out = jnp.sum(
        returned.astype(jnp.float32).reshape(EXPERTS, group, slot_count, width_dev), axis=1
    )
    mixed = jnp.einsum("est,esd->td", weighted, expert_out, precision=lax.Precision.HIGHEST)
    return mixed.astype(jnp.bfloat16)


def swap(value, expert_bits, hidden_bits):
    pairs = [
        (e * 4 + h, (e ^ expert_bits) * 4 + (h ^ hidden_bits)) for e in range(4) for h in range(4)
    ]
    return lax.ppermute(value, JOINT, pairs)


def in_vmem(array):
    return pltpu.with_memory_space_constraint(array, pltpu.VMEM)


def in_hbm(array):
    return pltpu.with_memory_space_constraint(array, pltpu.HBM)


def pack_body(tokens, router, routes, slots, out_ref, tok_ref, rw_ref, routes_ref, slots_ref, sem):
    rows, width = tok_ref.shape
    base = lax.axis_index("expert") * rows
    moves = ((tokens, tok_ref), (router, rw_ref), (routes, routes_ref), (slots, slots_ref))
    copies = [pltpu.make_async_copy(*move, sem.at[index]) for index, move in enumerate(moves)]
    for copy in copies:
        copy.start()
    for copy in copies:
        copy.wait()
    out_ref[:, :width] = tok_ref[...]
    values = tok_ref[...].astype(F32)
    lane = lax.broadcasted_iota(jnp.int32, (rows, LANES), 1)
    diagonal = lax.broadcasted_iota(jnp.int32, (rows, rows), 0) == lax.broadcasted_iota(
        jnp.int32, (rows, rows), 1
    )
    meta = jnp.zeros((rows, LANES), F32)
    for expert in range(EXPERTS):
        logit = jnp.sum(values * rw_ref[expert : expert + 1, :], axis=1, keepdims=True)
        high = logit.astype(BF16).astype(F32)
        middle = (logit - high).astype(BF16).astype(F32)
        low = logit - high - middle
        code = jnp.zeros((1, rows), F32) - 1.0
        for pick in range(2):
            here = (slots_ref[pick : pick + 1, :] - base).astype(F32)
            code = jnp.where(routes_ref[pick : pick + 1, :] == expert, here, code)
        column = jnp.sum(jnp.where(diagonal, code, 0.0), axis=1, keepdims=True)
        for place, term in enumerate((column, high, middle, low)):
            meta = jnp.where(lane == place * EXPERTS + expert, term, meta)
    out_ref[:, width:] = meta.astype(BF16)


PACK_FLOPS = 12_000_000_000


def pack(tokens, router_t, routes_t, slots_t):
    rows, width = tokens.shape
    arrays = [in_hbm(array) for array in (tokens, router_t, routes_t, slots_t)]
    return pl.pallas_call(
        pack_body,
        in_specs=[HBM] * 4,
        out_specs=VMEM,
        out_shape=pltpu.VMEM((rows, width + LANES), BF16),
        scratch_shapes=[pltpu.VMEM(array.shape, array.dtype) for array in arrays]
        + [pltpu.SemaphoreType.DMA((4,))],
        compiler_params=pltpu.CompilerParams(vmem_limit_bytes=4 * MIB),
        cost_estimate=pl.CostEstimate(flops=PACK_FLOPS, bytes_accessed=0, transcendentals=0),
        name="pack",
    )(*arrays)


def join_body(*refs):
    out_ref = refs[-1]
    rows = refs[0].shape[0]
    for index, ref in enumerate(refs[:-1]):
        out_ref[index * rows : (index + 1) * rows, :] = ref[...]


def join(parts):
    rows, width = parts[0].shape
    return pl.pallas_call(
        join_body,
        in_specs=[VMEM] * len(parts),
        out_specs=VMEM,
        out_shape=pltpu.VMEM((rows * len(parts), width), BF16),
        compiler_params=pltpu.CompilerParams(vmem_limit_bytes=4 * MIB),
        name="join",
    )(*parts)


def place():
    hidden = lax.axis_index("hidden")
    return hidden // 2, hidden % 2


TILE = 512


def span(index, size):
    return pl.ds(pl.multiple_of(index * size, size), size)


def fill_left(left, first, second, core, width):
    left[:, pl.ds(pl.multiple_of(core * width, LANES), width)] = first[:, :width]
    left[:, pl.ds(pl.multiple_of((1 - core) * width, LANES), width)] = second[:, :width]


FETCH_COST = pl.CostEstimate(flops=5_000_000_000, bytes_accessed=0, transcendentals=0)
SCOPE = 18 * MIB
SLOTS = 4
CUT = 512
SUB = 256


def fetch_body(wu, out, sem):
    chip, _ = place()
    copy = pltpu.make_async_copy(wu.at[0, span(chip, out.shape[0])], out, sem)
    copy.start()
    copy.wait()


def fetch(wu):
    return pl.pallas_call(
        fetch_body,
        in_specs=[HBM],
        out_specs=VMEM,
        out_shape=pltpu.VMEM((wu.shape[1] // 2, wu.shape[2]), BF16),
        scratch_shapes=[pltpu.SemaphoreType.DMA],
        cost_estimate=FETCH_COST,
        compiler_params=pltpu.CompilerParams(vmem_limit_bytes=SCOPE),
        name="fetch",
    )(wu)


def near_body(own, mate, expo, wg, up_near, wu, acc_g, acc_u, limits, up_far, left, sem):
    chip, core = place()
    rows = own.shape[0]
    width = own.shape[1] - LANES
    depth = 2 * width
    fill_left(left, own, mate, core, width)
    copies = []
    for index in range(up_near.shape[1] // TILE):
        columns = slice(index * TILE, (index + 1) * TILE)
        acc_u[:, columns] = jnp.dot(left[...], up_near[:, columns], preferred_element_type=F32)
        there = wu.at[0, span(1 - chip, depth), pl.ds(index * TILE, TILE)]
        copies.append(pltpu.make_async_copy(there, up_far.at[:, columns], sem.at[index]))
        copies[-1].start()
        acc_g[:, columns] = jnp.dot(
            left[...], wg[span(chip, depth), columns], preferred_element_type=F32
        )

    expert = lax.axis_index("expert")
    meta = own[:, width:].astype(F32)
    lane = lax.broadcasted_iota(jnp.int32, meta.shape, 1)
    code = jnp.sum(jnp.where(lane == expert, meta, 0.0), axis=1, keepdims=True)
    slots_each = rows // EXPERTS
    row = lax.broadcasted_iota(jnp.int32, (rows, rows), 0)
    source = jnp.bitwise_xor(row // slots_each, expert)
    target = jnp.where(code >= 0.0, (source * slots_each).astype(F32) + code, -1.0)
    chosen = lax.broadcasted_iota(jnp.int32, (rows, rows), 1).astype(F32) == target
    table = 448.0 * jnp.exp2(-expo[...].astype(F32))
    limits[...] = lax.dot_general(
        chosen.astype(BF16), table.astype(BF16), (((1,), (1,)), ((), ())), preferred_element_type=F32
    )
    for copy in copies:
        copy.wait()


def near(own, mate, expo, wg, up_near, wu):
    rows = own.shape[0]
    depth, units = up_near.shape
    acc = pltpu.VMEM((rows, units), F32)
    return pl.pallas_call(
        near_body,
        in_specs=[VMEM] * 5 + [HBM],
        out_specs=[VMEM] * 4,
        out_shape=[acc, acc, pltpu.VMEM((rows, expo.shape[0]), F32), pltpu.VMEM((depth, units), BF16)],
        input_output_aliases={4: 3},
        scratch_shapes=[
            pltpu.VMEM((rows, depth), BF16),
            pltpu.SemaphoreType.DMA((units // TILE,)),
        ],
        cost_estimate=pl.CostEstimate(
            flops=4 * rows * depth * units, bytes_accessed=2 * depth * units, transcendentals=0
        ),
        compiler_params=pltpu.CompilerParams(vmem_limit_bytes=SCOPE),
        name="near",
    )(own, mate, expo, wg, up_near, wu)


def far_body(
    own, mate, cross, cross_mate, expo, acc_g, acc_u, limits, up_far, wg, wd, send, keep,
    left, partial, buf, sem,
):
    del expo
    chip, core = place()
    expert = lax.axis_index("expert")
    rows = own.shape[0]
    width = own.shape[1] - LANES
    depth = 2 * width
    slots = buf.shape[0]
    cuts = wd.shape[1] // CUT

    def copy(unit):
        part = wd.at[0, pl.ds(unit * CUT, CUT)]
        return pltpu.make_async_copy(part, buf.at[unit % slots], sem.at[unit % slots])

    for unit in range(slots):
        copy(unit).start()
    fill_left(left, cross, cross_mate, core, width)

    meta = own[:, width:].astype(F32)
    lane = lax.broadcasted_iota(jnp.int32, meta.shape, 1)
    terms = meta
    for ref in (mate, cross, cross_mate):
        terms = terms + ref[:, width:].astype(F32)
    code = jnp.sum(jnp.where(lane == expert, meta, 0.0), axis=1, keepdims=True)
    first = jnp.zeros((rows, 1), F32)
    other = jnp.zeros((rows, 1), F32)
    for index in range(EXPERTS):
        used = (lane >= EXPERTS) & (lane < 4 * EXPERTS) & (lax.rem(lane, EXPERTS) == index)
        logit = jnp.sum(jnp.where(used, terms, 0.0), axis=1, keepdims=True)
        routed = meta[:, index : index + 1] >= 0.0
        first = jnp.where(index == expert, logit, first)
        other = jnp.where(routed & (index != expert), logit, other)
    weight = jnp.where(code >= 0.0, 1.0 / (1.0 + jnp.exp(other - first)), 0.0)

    for unit in range(cuts):
        pieces = []
        for sub in range(unit * CUT // SUB, (unit + 1) * CUT // SUB):
            columns = slice(sub * SUB, (sub + 1) * SUB)
            gate = acc_g[:, columns] + jnp.dot(
                left[...], wg[span(1 - chip, depth), columns], preferred_element_type=F32
            )
            up = acc_u[:, columns] + jnp.dot(
                left[...], up_far[:, columns], preferred_element_type=F32
            )
            pieces.append((gate / (1.0 + jnp.exp(-gate)) * up).astype(BF16))
        hidden = jnp.concatenate(pieces, axis=1)
        copy(unit).wait()
        term = jnp.dot(hidden, buf[unit % slots], preferred_element_type=F32)
        partial[...] = term if unit == 0 else partial[...] + term
        if unit + slots < cuts:
            copy(unit + slots).start()

    blocks = lax.broadcasted_iota(jnp.int32, limits.shape, 1)
    for block in range(4):
        to_chip = chip if block % 2 == 0 else 1 - chip
        owner = 2 * to_chip + (1 - core if block < 2 else core)
        sums = partial[:, span(owner, width)]
        out = (send, keep)[block // 2]
        for piece in range(width // LANES):
            columns = slice(piece * LANES, (piece + 1) * LANES)
            feature = owner * (width // LANES) + piece
            bound = jnp.sum(jnp.where(blocks == feature, limits[...], 0.0), axis=1, keepdims=True)
            coded = jnp.clip(sums[:, columns], -bound, bound).astype(BF16).astype(F32)
            out[block % 2, :, columns] = (coded * weight).astype(out.dtype)


def far(own, mate, cross, cross_mate, expo, acc_g, acc_u, limits, up_far, wg, wd):
    rows = own.shape[0]
    depth, units = up_far.shape
    width = depth // 2
    return pl.pallas_call(
        far_body,
        in_specs=[VMEM] * 10 + [HBM],
        out_specs=[VMEM, VMEM],
        out_shape=[pltpu.VMEM((2, rows, width), BF16), pltpu.VMEM((2, rows, width), F32)],
        scratch_shapes=[
            pltpu.VMEM((rows, depth), BF16),
            pltpu.VMEM((rows, wd.shape[2]), F32),
            pltpu.VMEM((SLOTS, CUT, wd.shape[2]), BF16),
            pltpu.SemaphoreType.DMA((SLOTS,)),
        ],
        cost_estimate=pl.CostEstimate(
            flops=8 * rows * depth * units, bytes_accessed=4 * depth * units, transcendentals=0
        ),
        compiler_params=pltpu.CompilerParams(vmem_limit_bytes=SCOPE),
        name="far",
    )(own, mate, cross, cross_mate, expo, acc_g, acc_u, limits, up_far, wg, wd)


def split_body(keep, got, *outs):
    rows = outs[0].shape[0]
    for index, out in enumerate(outs):
        chip, block = index // EXPERTS, index % EXPERTS
        piece = slice(block * rows, (block + 1) * rows)
        out[...] = (keep[chip, piece, :] + got[chip, piece, :].astype(F32)).astype(out.dtype)


def split(keep, got):
    rows, width = keep.shape[1] // EXPERTS, keep.shape[2]
    kinds = [F32] + [BF16] * (2 * EXPERTS - 1)
    return pl.pallas_call(
        split_body,
        in_specs=[VMEM, VMEM],
        out_specs=[VMEM] * len(kinds),
        out_shape=[jax.ShapeDtypeStruct((rows, width), kind) for kind in kinds],
        compiler_params=pltpu.CompilerParams(vmem_limit_bytes=4 * MIB),
        name="split",
    )(keep, got)


def total_body(*refs):
    total = refs[0][...]
    for ref in refs[1:-1]:
        total = total + ref[...].astype(F32)
    refs[-1][...] = total.astype(BF16)


def total(parts):
    return pl.pallas_call(
        total_body,
        in_specs=[VMEM] * len(parts),
        out_specs=VMEM,
        out_shape=jax.ShapeDtypeStruct(parts[0].shape, BF16),
        compiler_params=pltpu.CompilerParams(vmem_limit_bytes=4 * MIB),
        name="total",
    )(*parts)


RETURNS = ((1, 2), (1, 0), (0, 2), (3, 2), (3, 0), (2, 2), (2, 0))


def fast(tokens, router_weight, routes, slots, gate_weight, up_weight, down_weight, scale_exponents):
    packed = pack(tokens, router_weight.T, routes.T, slots.T)
    up_weight = in_hbm(up_weight)
    wg = in_vmem(gate_weight[0])
    arrived = [swap(packed, bits, 0) for bits in (1, 2, 3)]
    packed, up_near = lax.optimization_barrier((packed, fetch(up_weight)))
    own = in_vmem(join([packed] + arrived))
    mate = in_vmem(swap(own, 0, 1))
    cross = swap(own, 0, 2)
    expo = in_vmem(scale_exponents[0, 0].T)
    held = near(own, mate, expo, wg, in_vmem(up_near), up_weight)
    cross, *held = lax.optimization_barrier((cross, *held))
    cross = in_vmem(cross)
    cross_mate = in_vmem(swap(cross, 0, 1))
    send, keep = far(
        own, mate, cross, cross_mate, expo, *map(in_vmem, held), wg, in_hbm(down_weight)
    )
    blocks = split(in_vmem(keep), in_vmem(swap(send, 0, 1)))
    parts = [blocks[0]]
    for bits, chip in RETURNS:
        parts.append(swap(blocks[(chip // 2) * EXPERTS + bits], bits, chip))
    return total(parts)


def solution(mesh):
    placed = (
        P(("groups", "expert"), "hidden"),
        P("hidden", None),
        P(("groups", "expert"), None),
        P(("groups", "expert"), None),
        P("expert", None, "hidden"),
        P("expert", None, "hidden"),
        P("expert", "hidden", None),
        P(("groups", "expert"), "hidden", None, None),
    )
    general = mesh.shape["expert"] != 4 or mesh.shape["hidden"] != 4
    return jax.shard_map(
        on_device if general else fast,
        mesh=mesh,
        in_specs=placed,
        out_specs=P(("groups", "expert"), "hidden"),
        check_vma=False,
    )
```

```python
import functools

import jax
import jax.numpy as jnp
from jax import lax
from jax.experimental import pallas as pl
from jax.experimental.pallas import tpu as pltpu
from jax.sharding import PartitionSpec as P

EXPERTS = 4
LANES = 128
BF16 = jnp.bfloat16
F32 = jnp.float32
MIB = 1 << 20
JOINT = ("expert", "hidden")
VMEM = pl.BlockSpec(memory_space=pltpu.VMEM)
HBM = pl.BlockSpec(memory_space=pltpu.HBM)


def on_device(
    tokens, router_weight, routes, slots, gate_weight, up_weight, down_weight, scale_exponents
):
    slot_count = tokens.shape[0]
    width_dev = tokens.shape[1]
    group = lax.axis_size("expert") // EXPERTS
    source = lax.axis_index("expert")
    partial_logits = jnp.dot(
        tokens.astype(jnp.float32), router_weight, precision=lax.Precision.HIGHEST
    )
    logits = lax.psum(partial_logits, "hidden")
    expert_ids = jnp.arange(EXPERTS, dtype=jnp.int32)
    picked = (routes[:, :, None] == expert_ids[None, None, :]).astype(jnp.float32)
    chosen = jnp.sum(picked * logits[:, None, :], axis=2)
    first_w = jax.nn.sigmoid(chosen[:, 0] - chosen[:, 1])
    second_w = jax.nn.sigmoid(chosen[:, 1] - chosen[:, 0])
    route_w = jnp.stack([first_w, second_w], axis=1)
    local = slots - source * slot_count
    positions = jnp.arange(slot_count, dtype=jnp.int32)
    placed = (local[:, :, None] == positions[None, None, :]).astype(jnp.float32)
    select = jnp.einsum("tke,tks->est", picked, placed).astype(jnp.bfloat16)
    weighted = jnp.einsum("tke,tks,tk->est", picked, placed, route_w)
    gate_w = gate_weight[0]
    up_w = up_weight[0]
    whole = lax.all_gather(tokens, "hidden", axis=1, tiled=True)
    outgoing = jnp.einsum("est,td->esd", select, whole, preferred_element_type=jnp.float32).astype(
        jnp.bfloat16
    )
    outgoing = jnp.repeat(outgoing, group, axis=0)
    arrived = lax.all_to_all(outgoing, "expert", split_axis=0, concat_axis=0, tiled=True)
    rows_in = arrived.reshape(-1, arrived.shape[2])
    gate = jnp.dot(rows_in, gate_w, preferred_element_type=jnp.float32)
    up_val = jnp.dot(rows_in, up_w, preferred_element_type=jnp.float32)
    hidden = (jax.nn.silu(gate) * up_val).astype(jnp.bfloat16)
    partial_value = jnp.dot(hidden, down_weight[0], preferred_element_type=jnp.float32)
    capacity = partial_value.shape[0]
    features = partial_value.shape[1]
    limit = 448.0 * jnp.exp2(-scale_exponents[0, 0].astype(jnp.float32))[:, :, None]
    coded = jnp.clip(partial_value.reshape(capacity, features // 128, 128), -limit, limit).astype(
        jnp.bfloat16
    )
    coded = coded.reshape(capacity, features)
    summed = lax.psum_scatter(
        coded.astype(jnp.float32).astype(jnp.bfloat16), "hidden", scatter_dimension=1, tiled=True
    )
    quarter_out = summed.reshape(-1, slot_count, width_dev)
    returned = lax.all_to_all(quarter_out, "expert", split_axis=0, concat_axis=0, tiled=True)
    expert_out = jnp.sum(
        returned.astype(jnp.float32).reshape(EXPERTS, group, slot_count, width_dev), axis=1
    )
    mixed = jnp.einsum("est,esd->td", weighted, expert_out, precision=lax.Precision.HIGHEST)
    return mixed.astype(jnp.bfloat16)


def swap(value, expert_bits, hidden_bits):
    pairs = [
        (e * 4 + h, (e ^ expert_bits) * 4 + (h ^ hidden_bits)) for e in range(4) for h in range(4)
    ]
    return lax.ppermute(value, JOINT, pairs)


def in_vmem(array):
    return pltpu.with_memory_space_constraint(array, pltpu.VMEM)


def in_hbm(array):
    return pltpu.with_memory_space_constraint(array, pltpu.HBM)


def pack_body(tokens, router, routes, slots, out_ref, tok_ref, rw_ref, routes_ref, slots_ref, sem):
    rows, width = tok_ref.shape
    base = lax.axis_index("expert") * rows
    moves = ((tokens, tok_ref), (router, rw_ref), (routes, routes_ref), (slots, slots_ref))
    copies = [pltpu.make_async_copy(*move, sem.at[index]) for index, move in enumerate(moves)]
    for copy in copies:
        copy.start()
    for copy in copies:
        copy.wait()
    out_ref[:, :width] = tok_ref[...]
    values = tok_ref[...].astype(F32)
    lane = lax.broadcasted_iota(jnp.int32, (rows, LANES), 1)
    diagonal = lax.broadcasted_iota(jnp.int32, (rows, rows), 0) == lax.broadcasted_iota(
        jnp.int32, (rows, rows), 1
    )
    meta = jnp.zeros((rows, LANES), F32)
    for expert in range(EXPERTS):
        logit = jnp.sum(values * rw_ref[expert : expert + 1, :], axis=1, keepdims=True)
        high = logit.astype(BF16).astype(F32)
        middle = (logit - high).astype(BF16).astype(F32)
        low = logit - high - middle
        code = jnp.zeros((1, rows), F32) - 1.0
        for pick in range(2):
            here = (slots_ref[pick : pick + 1, :] - base).astype(F32)
            code = jnp.where(routes_ref[pick : pick + 1, :] == expert, here, code)
        column = jnp.sum(jnp.where(diagonal, code, 0.0), axis=1, keepdims=True)
        for place, term in enumerate((column, high, middle, low)):
            meta = jnp.where(lane == place * EXPERTS + expert, term, meta)
    out_ref[:, width:] = meta.astype(BF16)


PACK_FLOPS = 12_000_000_000


def pack(tokens, router_t, routes_t, slots_t):
    rows, width = tokens.shape
    arrays = [in_hbm(array) for array in (tokens, router_t, routes_t, slots_t)]
    return pl.pallas_call(
        pack_body,
        in_specs=[HBM] * 4,
        out_specs=VMEM,
        out_shape=pltpu.VMEM((rows, width + LANES), BF16),
        scratch_shapes=[pltpu.VMEM(array.shape, array.dtype) for array in arrays]
        + [pltpu.SemaphoreType.DMA((4,))],
        compiler_params=pltpu.CompilerParams(vmem_limit_bytes=4 * MIB),
        cost_estimate=pl.CostEstimate(flops=PACK_FLOPS, bytes_accessed=0, transcendentals=0),
        name="pack",
    )(*arrays)


def join_body(*refs):
    out_ref = refs[-1]
    rows = refs[0].shape[0]
    for index, ref in enumerate(refs[:-1]):
        out_ref[index * rows : (index + 1) * rows, :] = ref[...]


def join(parts):
    rows, width = parts[0].shape
    return pl.pallas_call(
        join_body,
        in_specs=[VMEM] * len(parts),
        out_specs=VMEM,
        out_shape=pltpu.VMEM((rows * len(parts), width), BF16),
        compiler_params=pltpu.CompilerParams(vmem_limit_bytes=4 * MIB),
        name="join",
    )(*parts)


def place():
    hidden = lax.axis_index("hidden")
    return hidden // 2, hidden % 2


TILE = 512


def span(index, size):
    return pl.ds(pl.multiple_of(index * size, size), size)


def fill_left(left, first, second, core, width):
    left[:, pl.ds(pl.multiple_of(core * width, LANES), width)] = first[:, :width]
    left[:, pl.ds(pl.multiple_of((1 - core) * width, LANES), width)] = second[:, :width]


FETCH_COST = pl.CostEstimate(flops=5_000_000_000, bytes_accessed=0, transcendentals=0)
SCOPE = 18 * MIB
SLOTS = 4
CUT = 512
SUB = 512


def fetch_body(wu, out, sem):
    chip, _ = place()
    copy = pltpu.make_async_copy(wu.at[0, span(chip, out.shape[0])], out, sem)
    copy.start()
    copy.wait()


def fetch(wu):
    return pl.pallas_call(
        fetch_body,
        in_specs=[HBM],
        out_specs=VMEM,
        out_shape=pltpu.VMEM((wu.shape[1] // 2, wu.shape[2]), BF16),
        scratch_shapes=[pltpu.SemaphoreType.DMA],
        cost_estimate=FETCH_COST,
        compiler_params=pltpu.CompilerParams(vmem_limit_bytes=SCOPE),
        name="fetch",
    )(wu)


def near_body(own, mate, expo, wg, up_near, wu, acc_g, acc_u, limits, up_far, left, sem):
    chip, core = place()
    rows = own.shape[0]
    width = own.shape[1] - LANES
    depth = 2 * width
    fill_left(left, own, mate, core, width)
    copies = []
    for index in range(up_near.shape[1] // TILE):
        columns = slice(index * TILE, (index + 1) * TILE)
        acc_u[:, columns] = jnp.dot(left[...], up_near[:, columns], preferred_element_type=F32)
        there = wu.at[0, span(1 - chip, depth), pl.ds(index * TILE, TILE)]
        copies.append(pltpu.make_async_copy(there, up_far.at[:, columns], sem.at[index]))
        copies[-1].start()
        acc_g[:, columns] = jnp.dot(
            left[...], wg[span(chip, depth), columns], preferred_element_type=F32
        )

    expert = lax.axis_index("expert")
    meta = own[:, width:].astype(F32)
    lane = lax.broadcasted_iota(jnp.int32, meta.shape, 1)
    code = jnp.sum(jnp.where(lane == expert, meta, 0.0), axis=1, keepdims=True)
    slots_each = rows // EXPERTS
    row = lax.broadcasted_iota(jnp.int32, (rows, rows), 0)
    source = jnp.bitwise_xor(row // slots_each, expert)
    target = jnp.where(code >= 0.0, (source * slots_each).astype(F32) + code, -1.0)
    chosen = lax.broadcasted_iota(jnp.int32, (rows, rows), 1).astype(F32) == target
    table = 448.0 * jnp.exp2(-expo[...].astype(F32))
    limits[...] = lax.dot_general(
        chosen.astype(BF16), table.astype(BF16), (((1,), (1,)), ((), ())), preferred_element_type=F32
    )
    for copy in copies:
        copy.wait()


def near(own, mate, expo, wg, up_near, wu):
    rows = own.shape[0]
    depth, units = up_near.shape
    acc = pltpu.VMEM((rows, units), F32)
    return pl.pallas_call(
        near_body,
        in_specs=[VMEM] * 5 + [HBM],
        out_specs=[VMEM] * 4,
        out_shape=[acc, acc, pltpu.VMEM((rows, expo.shape[0]), F32), pltpu.VMEM((depth, units), BF16)],
        input_output_aliases={4: 3},
        scratch_shapes=[
            pltpu.VMEM((rows, depth), BF16),
            pltpu.SemaphoreType.DMA((units // TILE,)),
        ],
        cost_estimate=pl.CostEstimate(
            flops=4 * rows * depth * units, bytes_accessed=2 * depth * units, transcendentals=0
        ),
        compiler_params=pltpu.CompilerParams(vmem_limit_bytes=SCOPE),
        name="near",
    )(own, mate, expo, wg, up_near, wu)


def far_body(
    own, mate, cross, cross_mate, expo, acc_g, acc_u, limits, up_far, wg, wd, send, keep,
    left, partial, buf, sem,
):
    del expo
    chip, core = place()
    expert = lax.axis_index("expert")
    rows = own.shape[0]
    width = own.shape[1] - LANES
    depth = 2 * width
    slots = buf.shape[0]
    cuts = wd.shape[1] // CUT

    def copy(unit):
        part = wd.at[0, pl.ds(unit * CUT, CUT)]
        return pltpu.make_async_copy(part, buf.at[unit % slots], sem.at[unit % slots])

    for unit in range(slots):
        copy(unit).start()
    fill_left(left, cross, cross_mate, core, width)

    meta = own[:, width:].astype(F32)
    lane = lax.broadcasted_iota(jnp.int32, meta.shape, 1)
    terms = meta
    for ref in (mate, cross, cross_mate):
        terms = terms + ref[:, width:].astype(F32)
    code = jnp.sum(jnp.where(lane == expert, meta, 0.0), axis=1, keepdims=True)
    first = jnp.zeros((rows, 1), F32)
    other = jnp.zeros((rows, 1), F32)
    for index in range(EXPERTS):
        used = (lane >= EXPERTS) & (lane < 4 * EXPERTS) & (lax.rem(lane, EXPERTS) == index)
        logit = jnp.sum(jnp.where(used, terms, 0.0), axis=1, keepdims=True)
        routed = meta[:, index : index + 1] >= 0.0
        first = jnp.where(index == expert, logit, first)
        other = jnp.where(routed & (index != expert), logit, other)
    weight = jnp.where(code >= 0.0, 1.0 / (1.0 + jnp.exp(other - first)), 0.0)

    for unit in range(cuts):
        pieces = []
        for sub in range(unit * CUT // SUB, (unit + 1) * CUT // SUB):
            columns = slice(sub * SUB, (sub + 1) * SUB)
            gate = acc_g[:, columns] + jnp.dot(
                left[...], wg[span(1 - chip, depth), columns], preferred_element_type=F32
            )
            up = acc_u[:, columns] + jnp.dot(
                left[...], up_far[:, columns], preferred_element_type=F32
            )
            pieces.append((gate / (1.0 + jnp.exp(-gate)) * up).astype(BF16))
        hidden = jnp.concatenate(pieces, axis=1)
        copy(unit).wait()
        term = jnp.dot(hidden, buf[unit % slots], preferred_element_type=F32)
        partial[...] = term if unit == 0 else partial[...] + term
        if unit + slots < cuts:
            copy(unit + slots).start()

    blocks = lax.broadcasted_iota(jnp.int32, limits.shape, 1)
    for block in range(4):
        to_chip = chip if block % 2 == 0 else 1 - chip
        owner = 2 * to_chip + (1 - core if block < 2 else core)
        sums = partial[:, span(owner, width)]
        out = (send, keep)[block // 2]
        for piece in range(width // LANES):
            columns = slice(piece * LANES, (piece + 1) * LANES)
            feature = owner * (width // LANES) + piece
            bound = jnp.sum(jnp.where(blocks == feature, limits[...], 0.0), axis=1, keepdims=True)
            coded = jnp.clip(sums[:, columns], -bound, bound).astype(BF16).astype(F32)
            out[block % 2, :, columns] = (coded * weight).astype(out.dtype)


def far(own, mate, cross, cross_mate, expo, acc_g, acc_u, limits, up_far, wg, wd):
    rows = own.shape[0]
    depth, units = up_far.shape
    width = depth // 2
    return pl.pallas_call(
        far_body,
        in_specs=[VMEM] * 10 + [HBM],
        out_specs=[VMEM, VMEM],
        out_shape=[pltpu.VMEM((2, rows, width), BF16), pltpu.VMEM((2, rows, width), F32)],
        scratch_shapes=[
            pltpu.VMEM((rows, depth), BF16),
            pltpu.VMEM((rows, wd.shape[2]), F32),
            pltpu.VMEM((SLOTS, CUT, wd.shape[2]), BF16),
            pltpu.SemaphoreType.DMA((SLOTS,)),
        ],
        cost_estimate=pl.CostEstimate(
            flops=8 * rows * depth * units, bytes_accessed=4 * depth * units, transcendentals=0
        ),
        compiler_params=pltpu.CompilerParams(vmem_limit_bytes=SCOPE),
        name="far",
    )(own, mate, cross, cross_mate, expo, acc_g, acc_u, limits, up_far, wg, wd)


def split_body(keep, got, *outs):
    rows = outs[0].shape[0]
    for index, out in enumerate(outs):
        chip, block = index // EXPERTS, index % EXPERTS
        piece = slice(block * rows, (block + 1) * rows)
        out[...] = (keep[chip, piece, :] + got[chip, piece, :].astype(F32)).astype(out.dtype)


def split(keep, got):
    rows, width = keep.shape[1] // EXPERTS, keep.shape[2]
    kinds = [F32] + [BF16] * (2 * EXPERTS - 1)
    return pl.pallas_call(
        split_body,
        in_specs=[VMEM, VMEM],
        out_specs=[VMEM] * len(kinds),
        out_shape=[jax.ShapeDtypeStruct((rows, width), kind) for kind in kinds],
        compiler_params=pltpu.CompilerParams(vmem_limit_bytes=4 * MIB),
        name="split",
    )(keep, got)


def total_body(*refs):
    total = refs[0][...]
    for ref in refs[1:-1]:
        total = total + ref[...].astype(F32)
    refs[-1][...] = total.astype(BF16)


def total(parts):
    return pl.pallas_call(
        total_body,
        in_specs=[VMEM] * len(parts),
        out_specs=VMEM,
        out_shape=jax.ShapeDtypeStruct(parts[0].shape, BF16),
        compiler_params=pltpu.CompilerParams(vmem_limit_bytes=4 * MIB),
        name="total",
    )(*parts)


RETURNS = ((1, 2), (1, 0), (0, 2), (3, 2), (3, 0), (2, 2), (2, 0))


def fast(tokens, router_weight, routes, slots, gate_weight, up_weight, down_weight, scale_exponents):
    packed = pack(tokens, router_weight.T, routes.T, slots.T)
    up_weight = in_hbm(up_weight)
    wg = in_vmem(gate_weight[0])
    arrived = [swap(packed, bits, 0) for bits in (1, 2, 3)]
    packed, up_near = lax.optimization_barrier((packed, fetch(up_weight)))
    own = in_vmem(join([packed] + arrived))
    mate = in_vmem(swap(own, 0, 1))
    cross = swap(own, 0, 2)
    expo = in_vmem(scale_exponents[0, 0].T)
    held = near(own, mate, expo, wg, in_vmem(up_near), up_weight)
    cross, *held = lax.optimization_barrier((cross, *held))
    cross = in_vmem(cross)
    cross_mate = in_vmem(swap(cross, 0, 1))
    send, keep = far(
        own, mate, cross, cross_mate, expo, *map(in_vmem, held), wg, in_hbm(down_weight)
    )
    blocks = split(in_vmem(keep), in_vmem(swap(send, 0, 1)))
    parts = [blocks[0]]
    for bits, chip in RETURNS:
        parts.append(swap(blocks[(chip // 2) * EXPERTS + bits], bits, chip))
    return total(parts)


def solution(mesh):
    placed = (
        P(("groups", "expert"), "hidden"),
        P("hidden", None),
        P(("groups", "expert"), None),
        P(("groups", "expert"), None),
        P("expert", None, "hidden"),
        P("expert", None, "hidden"),
        P("expert", "hidden", None),
        P(("groups", "expert"), "hidden", None, None),
    )
    general = mesh.shape["expert"] != 4 or mesh.shape["hidden"] != 4
    return jax.shard_map(
        on_device if general else fast,
        mesh=mesh,
        in_specs=placed,
        out_specs=P(("groups", "expert"), "hidden"),
        check_vma=False,
    )
```

```python
import functools

import jax
import jax.numpy as jnp
from jax import lax
from jax.experimental import pallas as pl
from jax.experimental.pallas import tpu as pltpu
from jax.sharding import PartitionSpec as P

EXPERTS = 4
LANES = 128
BF16 = jnp.bfloat16
F32 = jnp.float32
MIB = 1 << 20
JOINT = ("expert", "hidden")
VMEM = pl.BlockSpec(memory_space=pltpu.VMEM)
HBM = pl.BlockSpec(memory_space=pltpu.HBM)


def on_device(
    tokens, router_weight, routes, slots, gate_weight, up_weight, down_weight, scale_exponents
):
    slot_count = tokens.shape[0]
    width_dev = tokens.shape[1]
    group = lax.axis_size("expert") // EXPERTS
    source = lax.axis_index("expert")
    partial_logits = jnp.dot(
        tokens.astype(jnp.float32), router_weight, precision=lax.Precision.HIGHEST
    )
    logits = lax.psum(partial_logits, "hidden")
    expert_ids = jnp.arange(EXPERTS, dtype=jnp.int32)
    picked = (routes[:, :, None] == expert_ids[None, None, :]).astype(jnp.float32)
    chosen = jnp.sum(picked * logits[:, None, :], axis=2)
    first_w = jax.nn.sigmoid(chosen[:, 0] - chosen[:, 1])
    second_w = jax.nn.sigmoid(chosen[:, 1] - chosen[:, 0])
    route_w = jnp.stack([first_w, second_w], axis=1)
    local = slots - source * slot_count
    positions = jnp.arange(slot_count, dtype=jnp.int32)
    placed = (local[:, :, None] == positions[None, None, :]).astype(jnp.float32)
    select = jnp.einsum("tke,tks->est", picked, placed).astype(jnp.bfloat16)
    weighted = jnp.einsum("tke,tks,tk->est", picked, placed, route_w)
    gate_w = gate_weight[0]
    up_w = up_weight[0]
    whole = lax.all_gather(tokens, "hidden", axis=1, tiled=True)
    outgoing = jnp.einsum("est,td->esd", select, whole, preferred_element_type=jnp.float32).astype(
        jnp.bfloat16
    )
    outgoing = jnp.repeat(outgoing, group, axis=0)
    arrived = lax.all_to_all(outgoing, "expert", split_axis=0, concat_axis=0, tiled=True)
    rows_in = arrived.reshape(-1, arrived.shape[2])
    gate = jnp.dot(rows_in, gate_w, preferred_element_type=jnp.float32)
    up_val = jnp.dot(rows_in, up_w, preferred_element_type=jnp.float32)
    hidden = (jax.nn.silu(gate) * up_val).astype(jnp.bfloat16)
    partial_value = jnp.dot(hidden, down_weight[0], preferred_element_type=jnp.float32)
    capacity = partial_value.shape[0]
    features = partial_value.shape[1]
    limit = 448.0 * jnp.exp2(-scale_exponents[0, 0].astype(jnp.float32))[:, :, None]
    coded = jnp.clip(partial_value.reshape(capacity, features // 128, 128), -limit, limit).astype(
        jnp.bfloat16
    )
    coded = coded.reshape(capacity, features)
    summed = lax.psum_scatter(
        coded.astype(jnp.float32).astype(jnp.bfloat16), "hidden", scatter_dimension=1, tiled=True
    )
    quarter_out = summed.reshape(-1, slot_count, width_dev)
    returned = lax.all_to_all(quarter_out, "expert", split_axis=0, concat_axis=0, tiled=True)
    expert_out = jnp.sum(
        returned.astype(jnp.float32).reshape(EXPERTS, group, slot_count, width_dev), axis=1
    )
    mixed = jnp.einsum("est,esd->td", weighted, expert_out, precision=lax.Precision.HIGHEST)
    return mixed.astype(jnp.bfloat16)


def swap(value, expert_bits, hidden_bits):
    pairs = [
        (e * 4 + h, (e ^ expert_bits) * 4 + (h ^ hidden_bits)) for e in range(4) for h in range(4)
    ]
    return lax.ppermute(value, JOINT, pairs)


def in_vmem(array):
    return pltpu.with_memory_space_constraint(array, pltpu.VMEM)


def in_hbm(array):
    return pltpu.with_memory_space_constraint(array, pltpu.HBM)


def pack_body(tokens, router, routes, slots, out_ref, tok_ref, rw_ref, routes_ref, slots_ref, sem):
    rows, width = tok_ref.shape
    base = lax.axis_index("expert") * rows
    moves = ((tokens, tok_ref), (router, rw_ref), (routes, routes_ref), (slots, slots_ref))
    copies = [pltpu.make_async_copy(*move, sem.at[index]) for index, move in enumerate(moves)]
    for copy in copies:
        copy.start()
    for copy in copies:
        copy.wait()
    out_ref[:, :width] = tok_ref[...]
    values = tok_ref[...].astype(F32)
    lane = lax.broadcasted_iota(jnp.int32, (rows, LANES), 1)
    diagonal = lax.broadcasted_iota(jnp.int32, (rows, rows), 0) == lax.broadcasted_iota(
        jnp.int32, (rows, rows), 1
    )
    meta = jnp.zeros((rows, LANES), F32)
    for expert in range(EXPERTS):
        logit = jnp.sum(values * rw_ref[expert : expert + 1, :], axis=1, keepdims=True)
        high = logit.astype(BF16).astype(F32)
        middle = (logit - high).astype(BF16).astype(F32)
        low = logit - high - middle
        code = jnp.zeros((1, rows), F32) - 1.0
        for pick in range(2):
            here = (slots_ref[pick : pick + 1, :] - base).astype(F32)
            code = jnp.where(routes_ref[pick : pick + 1, :] == expert, here, code)
        column = jnp.sum(jnp.where(diagonal, code, 0.0), axis=1, keepdims=True)
        for place, term in enumerate((column, high, middle, low)):
            meta = jnp.where(lane == place * EXPERTS + expert, term, meta)
    out_ref[:, width:] = meta.astype(BF16)


PACK_FLOPS = 12_000_000_000


def pack(tokens, router_t, routes_t, slots_t):
    rows, width = tokens.shape
    arrays = [in_hbm(array) for array in (tokens, router_t, routes_t, slots_t)]
    return pl.pallas_call(
        pack_body,
        in_specs=[HBM] * 4,
        out_specs=VMEM,
        out_shape=pltpu.VMEM((rows, width + LANES), BF16),
        scratch_shapes=[pltpu.VMEM(array.shape, array.dtype) for array in arrays]
        + [pltpu.SemaphoreType.DMA((4,))],
        compiler_params=pltpu.CompilerParams(vmem_limit_bytes=4 * MIB),
        cost_estimate=pl.CostEstimate(flops=PACK_FLOPS, bytes_accessed=0, transcendentals=0),
        name="pack",
    )(*arrays)


def join_body(*refs):
    out_ref = refs[-1]
    rows = refs[0].shape[0]
    for index, ref in enumerate(refs[:-1]):
        out_ref[index * rows : (index + 1) * rows, :] = ref[...]


def join(parts):
    rows, width = parts[0].shape
    return pl.pallas_call(
        join_body,
        in_specs=[VMEM] * len(parts),
        out_specs=VMEM,
        out_shape=pltpu.VMEM((rows * len(parts), width), BF16),
        compiler_params=pltpu.CompilerParams(vmem_limit_bytes=4 * MIB),
        name="join",
    )(*parts)


def place():
    hidden = lax.axis_index("hidden")
    return hidden // 2, hidden % 2


TILE = 512


def span(index, size):
    return pl.ds(pl.multiple_of(index * size, size), size)


def fill_left(left, first, second, core, width):
    left[:, pl.ds(pl.multiple_of(core * width, LANES), width)] = first[:, :width]
    left[:, pl.ds(pl.multiple_of((1 - core) * width, LANES), width)] = second[:, :width]


FETCH_COST = pl.CostEstimate(flops=5_000_000_000, bytes_accessed=0, transcendentals=0)
SCOPE = 16 * MIB
SLOTS = 3
CUT = 512
SUB = 512


def fetch_body(wu, out, sem):
    chip, _ = place()
    copy = pltpu.make_async_copy(wu.at[0, span(chip, out.shape[0])], out, sem)
    copy.start()
    copy.wait()


def fetch(wu):
    return pl.pallas_call(
        fetch_body,
        in_specs=[HBM],
        out_specs=VMEM,
        out_shape=pltpu.VMEM((wu.shape[1] // 2, wu.shape[2]), BF16),
        scratch_shapes=[pltpu.SemaphoreType.DMA],
        cost_estimate=FETCH_COST,
        compiler_params=pltpu.CompilerParams(vmem_limit_bytes=SCOPE),
        name="fetch",
    )(wu)


def near_body(
    own, mate, expo, wg, up_near, wu, wd, acc_g, acc_u, limits, up_far, down_first, left, sem
):
    chip, core = place()
    rows = own.shape[0]
    width = own.shape[1] - LANES
    depth = 2 * width
    slab = wd.at[0, pl.ds(0, down_first.shape[0])]
    copies = [pltpu.make_async_copy(slab, down_first, sem.at[up_near.shape[1] // TILE])]
    copies[0].start()
    fill_left(left, own, mate, core, width)
    for index in range(up_near.shape[1] // TILE):
        columns = slice(index * TILE, (index + 1) * TILE)
        acc_u[:, columns] = jnp.dot(left[...], up_near[:, columns], preferred_element_type=F32)
        there = wu.at[0, span(1 - chip, depth), pl.ds(index * TILE, TILE)]
        copies.append(pltpu.make_async_copy(there, up_far.at[:, columns], sem.at[index]))
        copies[-1].start()
        acc_g[:, columns] = jnp.dot(
            left[...], wg[span(chip, depth), columns], preferred_element_type=F32
        )

    expert = lax.axis_index("expert")
    meta = own[:, width:].astype(F32)
    lane = lax.broadcasted_iota(jnp.int32, meta.shape, 1)
    code = jnp.sum(jnp.where(lane == expert, meta, 0.0), axis=1, keepdims=True)
    slots_each = rows // EXPERTS
    row = lax.broadcasted_iota(jnp.int32, (rows, rows), 0)
    source = jnp.bitwise_xor(row // slots_each, expert)
    target = jnp.where(code >= 0.0, (source * slots_each).astype(F32) + code, -1.0)
    chosen = lax.broadcasted_iota(jnp.int32, (rows, rows), 1).astype(F32) == target
    table = 448.0 * jnp.exp2(-expo[...].astype(F32))
    limits[...] = lax.dot_general(
        chosen.astype(BF16), table.astype(BF16), (((1,), (1,)), ((), ())), preferred_element_type=F32
    )
    for copy in copies:
        copy.wait()


def near(own, mate, expo, wg, up_near, wu, wd):
    rows = own.shape[0]
    depth, units = up_near.shape
    acc = pltpu.VMEM((rows, units), F32)
    return pl.pallas_call(
        near_body,
        in_specs=[VMEM] * 5 + [HBM] * 2,
        out_specs=[VMEM] * 5,
        out_shape=[
            acc,
            acc,
            pltpu.VMEM((rows, expo.shape[0]), F32),
            pltpu.VMEM((depth, units), BF16),
            pltpu.VMEM((CUT, wd.shape[2]), BF16),
        ],
        input_output_aliases={4: 3},
        scratch_shapes=[
            pltpu.VMEM((rows, depth), BF16),
            pltpu.SemaphoreType.DMA((units // TILE + 1,)),
        ],
        cost_estimate=pl.CostEstimate(
            flops=4 * rows * depth * units, bytes_accessed=2 * depth * units, transcendentals=0
        ),
        compiler_params=pltpu.CompilerParams(vmem_limit_bytes=SCOPE),
        name="near",
    )(own, mate, expo, wg, up_near, wu, wd)


def far_body(
    own, mate, cross, cross_mate, expo, acc_g, acc_u, limits, up_far, down_first, wg, wd,
    send, keep,
    left, partial, buf, sem,
):
    del expo
    chip, core = place()
    expert = lax.axis_index("expert")
    rows = own.shape[0]
    width = own.shape[1] - LANES
    depth = 2 * width
    slots = buf.shape[0]
    cuts = wd.shape[1] // CUT

    def copy(unit):
        part = wd.at[0, pl.ds(unit * CUT, CUT)]
        return pltpu.make_async_copy(part, buf.at[unit % slots], sem.at[unit % slots])

    for unit in range(1, slots + 1):
        copy(unit).start()
    fill_left(left, cross, cross_mate, core, width)

    meta = own[:, width:].astype(F32)
    lane = lax.broadcasted_iota(jnp.int32, meta.shape, 1)
    terms = meta
    for ref in (mate, cross, cross_mate):
        terms = terms + ref[:, width:].astype(F32)
    code = jnp.sum(jnp.where(lane == expert, meta, 0.0), axis=1, keepdims=True)
    first = jnp.zeros((rows, 1), F32)
    other = jnp.zeros((rows, 1), F32)
    for index in range(EXPERTS):
        used = (lane >= EXPERTS) & (lane < 4 * EXPERTS) & (lax.rem(lane, EXPERTS) == index)
        logit = jnp.sum(jnp.where(used, terms, 0.0), axis=1, keepdims=True)
        routed = meta[:, index : index + 1] >= 0.0
        first = jnp.where(index == expert, logit, first)
        other = jnp.where(routed & (index != expert), logit, other)
    weight = jnp.where(code >= 0.0, 1.0 / (1.0 + jnp.exp(other - first)), 0.0)

    for unit in range(cuts):
        pieces = []
        for sub in range(unit * CUT // SUB, (unit + 1) * CUT // SUB):
            columns = slice(sub * SUB, (sub + 1) * SUB)
            gate = acc_g[:, columns] + jnp.dot(
                left[...], wg[span(1 - chip, depth), columns], preferred_element_type=F32
            )
            up = acc_u[:, columns] + jnp.dot(
                left[...], up_far[:, columns], preferred_element_type=F32
            )
            pieces.append((gate / (1.0 + jnp.exp(-gate)) * up).astype(BF16))
        hidden = jnp.concatenate(pieces, axis=1)
        if unit > 0:
            copy(unit).wait()
        slab = buf[unit % slots] if unit > 0 else down_first[...]
        term = jnp.dot(hidden, slab, preferred_element_type=F32)
        partial[...] = term if unit == 0 else partial[...] + term
        if 0 < unit < cuts - slots:
            copy(unit + slots).start()

    blocks = lax.broadcasted_iota(jnp.int32, limits.shape, 1)
    for block in range(4):
        to_chip = chip if block % 2 == 0 else 1 - chip
        owner = 2 * to_chip + (1 - core if block < 2 else core)
        sums = partial[:, span(owner, width)]
        out = (send, keep)[block // 2]
        for piece in range(width // LANES):
            columns = slice(piece * LANES, (piece + 1) * LANES)
            feature = owner * (width // LANES) + piece
            bound = jnp.sum(jnp.where(blocks == feature, limits[...], 0.0), axis=1, keepdims=True)
            coded = jnp.clip(sums[:, columns], -bound, bound).astype(BF16).astype(F32)
            out[block % 2, :, columns] = (coded * weight).astype(out.dtype)


def far(own, mate, cross, cross_mate, expo, acc_g, acc_u, limits, up_far, down_first, wg, wd):
    rows = own.shape[0]
    depth, units = up_far.shape
    width = depth // 2
    return pl.pallas_call(
        far_body,
        in_specs=[VMEM] * 11 + [HBM],
        out_specs=[VMEM, VMEM],
        out_shape=[pltpu.VMEM((2, rows, width), BF16), pltpu.VMEM((2, rows, width), F32)],
        scratch_shapes=[
            pltpu.VMEM((rows, depth), BF16),
            pltpu.VMEM((rows, wd.shape[2]), F32),
            pltpu.VMEM((SLOTS, CUT, wd.shape[2]), BF16),
            pltpu.SemaphoreType.DMA((SLOTS,)),
        ],
        cost_estimate=pl.CostEstimate(
            flops=8 * rows * depth * units, bytes_accessed=4 * depth * units, transcendentals=0
        ),
        compiler_params=pltpu.CompilerParams(vmem_limit_bytes=SCOPE),
        name="far",
    )(own, mate, cross, cross_mate, expo, acc_g, acc_u, limits, up_far, down_first, wg, wd)


def split_body(keep, got, *outs):
    rows = outs[0].shape[0]
    for index, out in enumerate(outs):
        chip, block = index // EXPERTS, index % EXPERTS
        piece = slice(block * rows, (block + 1) * rows)
        out[...] = (keep[chip, piece, :] + got[chip, piece, :].astype(F32)).astype(out.dtype)


def split(keep, got):
    rows, width = keep.shape[1] // EXPERTS, keep.shape[2]
    kinds = [F32] + [BF16] * (2 * EXPERTS - 1)
    return pl.pallas_call(
        split_body,
        in_specs=[VMEM, VMEM],
        out_specs=[VMEM] * len(kinds),
        out_shape=[jax.ShapeDtypeStruct((rows, width), kind) for kind in kinds],
        compiler_params=pltpu.CompilerParams(vmem_limit_bytes=4 * MIB),
        name="split",
    )(keep, got)


def total_body(*refs):
    total = refs[0][...]
    for ref in refs[1:-1]:
        total = total + ref[...].astype(F32)
    refs[-1][...] = total.astype(BF16)


def total(parts):
    return pl.pallas_call(
        total_body,
        in_specs=[VMEM] * len(parts),
        out_specs=VMEM,
        out_shape=jax.ShapeDtypeStruct(parts[0].shape, BF16),
        compiler_params=pltpu.CompilerParams(vmem_limit_bytes=4 * MIB),
        name="total",
    )(*parts)


RETURNS = ((1, 2), (1, 0), (0, 2), (3, 2), (3, 0), (2, 2), (2, 0))


def fast(tokens, router_weight, routes, slots, gate_weight, up_weight, down_weight, scale_exponents):
    packed = pack(tokens, router_weight.T, routes.T, slots.T)
    up_weight, down_weight = in_hbm(up_weight), in_hbm(down_weight)
    wg = in_vmem(gate_weight[0])
    arrived = [swap(packed, bits, 0) for bits in (1, 2, 3)]
    packed, up_near = lax.optimization_barrier((packed, fetch(up_weight)))
    own = in_vmem(join([packed] + arrived))
    mate = in_vmem(swap(own, 0, 1))
    cross = swap(own, 0, 2)
    expo = in_vmem(scale_exponents[0, 0].T)
    held = near(own, mate, expo, wg, in_vmem(up_near), up_weight, down_weight)
    cross, *held = lax.optimization_barrier((cross, *held))
    cross = in_vmem(cross)
    cross_mate = in_vmem(swap(cross, 0, 1))
    send, keep = far(
        own, mate, cross, cross_mate, expo, *map(in_vmem, held), wg, down_weight
    )
    blocks = split(in_vmem(keep), in_vmem(swap(send, 0, 1)))
    parts = [blocks[0]]
    for bits, chip in RETURNS:
        parts.append(swap(blocks[(chip // 2) * EXPERTS + bits], bits, chip))
    return total(parts)


def solution(mesh):
    placed = (
        P(("groups", "expert"), "hidden"),
        P("hidden", None),
        P(("groups", "expert"), None),
        P(("groups", "expert"), None),
        P("expert", None, "hidden"),
        P("expert", None, "hidden"),
        P("expert", "hidden", None),
        P(("groups", "expert"), "hidden", None, None),
    )
    general = mesh.shape["expert"] != 4 or mesh.shape["hidden"] != 4
    return jax.shard_map(
        on_device if general else fast,
        mesh=mesh,
        in_specs=placed,
        out_specs=P(("groups", "expert"), "hidden"),
        check_vma=False,
    )
```
